32 devices in a mesh: groups: 2 (over y), tensor: 4 (over z), request: 4 (over x, core).
Axes of the slice: x: 2, y: 2, z: 4, core: 2. Of those that a mesh axis runs over, the one named last changes fastest.
Arguments:
- q_nope: bfloat16 [1536, 16384], P(('groups', 'request'), 'tensor'), parts along dimension 0, may hold values from -6 to 6
- q_rope: bfloat16 [1536, 8192], P(('groups', 'request'), 'tensor'), parts along dimension 0, may hold values from -8 to 8
- latent_keys: bfloat16 [32, 512, 576], P(('groups', 'request'), 'tensor'), parts along dimension 0, may hold values from -8 to 8
- w_key: bfloat16 [128, 512, 128], P('tensor'), may hold values from -0.25 to 0.25
- w_value: bfloat16 [128, 512, 128], P('tensor'), may hold values from -4 to 4
- w_out: bfloat16 [16384, 7168], P('tensor', 'request'), may hold values from -0.046875 to 0.046875
- prefix_len: int32 [32], P(('groups', 'request')), parts along dimension 0, may hold values from 256 to 464
- stretch_len: int32 [32], P(('groups', 'request')), parts along dimension 0, may hold values from 12 to 48
- finished: int32 [32], P(('groups', 'request')), parts along dimension 0, may hold values 0 or 1
- owners: int32 [32, 4], P(('groups', 'request'), 'tensor'), parts along dimension 0, may hold values from 0 to 3, as said below
Outputs:
- mixed: bfloat16 [8, 192, 7168], P(('groups', 'request'), 'tensor'), parts along dimension 0
- handed: bfloat16 [8, 4, 512, 576], P(('groups', 'request'), None, 'tensor'), parts along dimension 0
The draws below stay inside these ranges and needn't reach their ends.
There are 2 independent parts, one for each index of `groups`. The reference program is written for one: setup_inputs(seed, part) draws one part's arguments, and reference() takes and returns one part's arrays. A program takes and returns all parts, laid end to end along the dimension named above; an argument that names none is the same for every part. Nothing has to cross between parts.
Inputs may be any that keep to these rules, and one draw needn't show every extreme that they name: For each block index, the 4 requests of one request rank name distinct owners.
All inputs are finite; a program needn't handle non-finite values. No bound on the sum of `finished` on one device may be relied on, other than what follows from the above.
Results may differ from the reference program's by a relative error of at most 0.012.
Values may be sent and summed in bfloat16 or wider, within the bound.
No kernel may reach another device: no remote copies, remote signals or barrier semaphores. Data moves between devices by JAX's collectives and lax.ppermute only.
A program may use at most 256 MiB of HBM per device.

```python
import jax
import jax.numpy as jnp
from jax import lax

D = 7168
HEADS = 128
LATENT = 512
ROPE = 64
NOPE = 128
VDIM = 128
BLOCK = 128
REQ_DEV = 4
STRETCH = 48
REQUESTS = 16
TOKENS = 768
SPAN = 512
N_REQUEST = 4


def draw_q_rope(key, part):
    key = jax.random.fold_in(key, 11)
    shape = (REQUESTS * STRETCH, HEADS * ROPE)
    values = jnp.clip(jax.random.normal(key, shape, jnp.float32), -8.0, 8.0)
    return values.astype(jnp.bfloat16)


def draw_latent_keys(key, part):
    key = jax.random.fold_in(key, 12)
    shape = (REQUESTS, SPAN, LATENT + ROPE)
    values = jnp.clip(jax.random.normal(key, shape, jnp.float32), -8.0, 8.0)
    return values.astype(jnp.bfloat16)


def spread_ends(key, low, high):
    values = jax.random.randint(jax.random.fold_in(key, 1), (REQUESTS,), low, high + 1)
    first = jax.random.randint(jax.random.fold_in(key, 2), (), 0, REQUESTS)
    second = (first + 1) % REQUESTS
    values = values.at[first].set(high)
    values = values.at[second].set(low)
    return values.astype(jnp.int32)


def draw_prefix_len(key, part):
    key = jax.random.fold_in(key, 13)
    return spread_ends(key, SPAN // 2, SPAN - STRETCH)


def draw_stretch_len(key, part):
    key = jax.random.fold_in(key, 14)
    return spread_ends(key, STRETCH // 4, STRETCH)


def draw_owners(key, part):
    key = jax.random.fold_in(key, 15)
    rank_count = REQUESTS // REQ_DEV
    block_count = SPAN // BLOCK
    scores = jax.random.randint(key, (rank_count, block_count, rank_count), 0, 1 << 20) * rank_count
    scores = scores + jnp.arange(rank_count, dtype=jnp.int32)[None, None, :]
    order = jnp.argsort(scores, axis=2).astype(jnp.int32)
    picked = order[:, :, :REQ_DEV]
    return jnp.transpose(picked, (0, 2, 1)).reshape(REQUESTS, block_count).astype(jnp.int32)


def with_ends(result, rng, smallest, largest):
    longest = result.shape.index(max(result.shape))
    spots = []
    for shift in (0, 1):
        where = [jax.random.randint(jax.random.fold_in(rng, axis), (), 0, length) for axis, length in enumerate(result.shape)]
        where[longest] = (where[longest] + shift) % result.shape[longest]
        spots.append(tuple(where))
    return result.at[spots[0]].set(smallest).at[spots[1]].set(largest)


def levels(stream_key, shape, shards, least, largest):
    factor_of = 1.0
    for position, shards_of in shards:
        heights = jax.random.uniform(jax.random.fold_in(jax.random.fold_in(stream_key, 6), position), (shards_of,), jnp.float32, least / len(shards), largest / len(shards))
        factor_of = factor_of * jnp.repeat(jnp.exp(heights), shape[position] // shards_of).reshape((-1,) + (1,) * (len(shape) - 1 - position))
    return factor_of


def scatter_about(stream_key, dims, deviation, bound, pieces=(), kind=jnp.bfloat16):
    level = levels(stream_key, dims, pieces, -0.22, 0.18) if pieces else 1.0
    entries = jax.random.normal(stream_key, dims, jnp.float32) * deviation * level
    return jnp.minimum(jnp.maximum(entries, -bound), bound).astype(kind)


def setup_inputs(seed: int = 0, part: int = 0) -> dict:
    key_of = jax.random.split(jax.random.key(seed), 11)
    part_keys = jax.random.split(jax.random.fold_in(key_of[10], part), 11)
    q_nope = scatter_about(part_keys[0], (TOKENS, HEADS * NOPE), 1.0, 6.0, ((0, 4), (1, 4)))
    q_rope = draw_q_rope(jax.random.fold_in(jax.random.fold_in(key_of[10], part), 71), part)
    latent_keys = draw_latent_keys(jax.random.fold_in(jax.random.fold_in(key_of[10], part), 71), part)
    w_key = scatter_about(key_of[3], (HEADS, LATENT, NOPE), LATENT ** -0.5, 0.25, ((0, 4),))
    w_value = scatter_about(key_of[4], (HEADS, LATENT, VDIM), (max(LATENT // 256, 1)) ** -0.5, 4.0, ((0, 4),))
    w_out = scatter_about(key_of[5], (HEADS * VDIM, D), (HEADS * VDIM) ** -0.5, 0.046875, ((0, 4), (1, 4)))
    prefix_len = draw_prefix_len(jax.random.fold_in(jax.random.fold_in(key_of[10], part), 71), part)
    stretch_len = draw_stretch_len(jax.random.fold_in(jax.random.fold_in(key_of[10], part), 71), part)
    finished = with_ends((jax.random.randint(part_keys[8], (REQUESTS,), 0, 8) < 7).astype(jnp.int32), jax.random.fold_in(part_keys[8], 1), 0, 1)
    owners = draw_owners(jax.random.fold_in(jax.random.fold_in(key_of[10], part), 71), part)
    return {"q_nope": q_nope, "q_rope": q_rope, "latent_keys": latent_keys, "w_key": w_key, "w_value": w_value, "w_out": w_out, "prefix_len": prefix_len, "stretch_len": stretch_len, "finished": finished, "owners": owners}


def reference(q_nope, q_rope, latent_keys, w_key, w_value, w_out, prefix_len, stretch_len, finished, owners):
    score_scale = (NOPE + ROPE) ** -0.5
    queries = q_nope.reshape(REQUESTS, STRETCH, HEADS, NOPE).astype(jnp.float32)
    absorbed = jnp.einsum("rihd,hcd->rihc", queries, w_key.astype(jnp.float32)).astype(jnp.bfloat16)
    rotary = q_rope.reshape(REQUESTS, STRETCH, HEADS, ROPE)
    full_query = lax.optimization_barrier(jnp.concatenate([absorbed, rotary], axis=3))

    def per_request(inputs):
        query_block, key_block, start_pos = inputs
        scores = jnp.einsum("ihc,jc->ihj", query_block.astype(jnp.float32), key_block.astype(jnp.float32)) * score_scale
        key_pos = jnp.arange(SPAN, dtype=jnp.int32)
        query_pos = start_pos + jnp.arange(STRETCH, dtype=jnp.int32)
        visible = key_pos[None, :] <= query_pos[:, None]
        scores = jnp.where(visible[:, None, :], scores, -jnp.inf)
        row_max = jnp.max(scores, axis=2, keepdims=True)
        weights = jnp.exp(scores - row_max)
        denom = jnp.sum(weights, axis=2)
        rounded = lax.optimization_barrier(weights.astype(jnp.bfloat16)).astype(jnp.float32)
        summed = jnp.einsum("ihj,jc->ihc", rounded, key_block[:, :LATENT].astype(jnp.float32))
        return (summed / denom[:, :, None]).astype(jnp.bfloat16)

    latent_out = lax.map(per_request, (full_query, latent_keys, prefix_len))
    latent_back = lax.optimization_barrier(latent_out).astype(jnp.float32)
    head_out = jnp.einsum("rihc,hcv->rihv", latent_back, w_value.astype(jnp.float32)).astype(jnp.bfloat16)
    live_rows = jnp.arange(STRETCH, dtype=jnp.int32)[None, :] < stretch_len[:, None]
    head_out = jnp.where(live_rows[:, :, None, None], head_out, jnp.zeros_like(head_out))
    head_rows = head_out.reshape(TOKENS, HEADS * VDIM)
    mixed = jnp.dot(head_rows, w_out, preferred_element_type=jnp.float32).astype(jnp.bfloat16)
    mixed = mixed.reshape(N_REQUEST, REQ_DEV * STRETCH, D)

    rank_count = N_REQUEST
    width_all = LATENT + ROPE
    grouped_keys = latent_keys.reshape(rank_count, REQ_DEV, SPAN, width_all).astype(jnp.float32)
    seq_ends = (prefix_len + stretch_len).reshape(rank_count, REQ_DEV)
    done_flags = finished.reshape(rank_count, REQ_DEV)
    owner_pos = jnp.repeat(owners, BLOCK, axis=1).reshape(rank_count, REQ_DEV, SPAN)
    positions = jnp.arange(SPAN, dtype=jnp.int32)
    live_keys = (positions[None, None, :] < seq_ends[:, :, None]) & (done_flags[:, :, None] > 0)

    def for_owner(target):
        picked = live_keys & (owner_pos == target)
        chosen = jnp.where(picked[:, :, :, None], grouped_keys, jnp.zeros_like(grouped_keys))
        return jnp.sum(chosen, axis=1).astype(jnp.bfloat16)

    handed = lax.map(for_owner, jnp.arange(rank_count, dtype=jnp.int32))
    return mixed, handed
```

```python
import jax
import jax.numpy as jnp
from jax import lax
from jax.sharding import PartitionSpec as P


def local(
    q_nope, q_rope, latent_keys, w_key, w_value, w_out, prefix_len, stretch_len, finished, owners
):
    request_count = prefix_len.shape[0]
    row_count = q_nope.shape[0]
    stretch_size = row_count // request_count
    head_count = w_key.shape[0]
    latent_width = w_key.shape[1]
    nope_width = w_key.shape[2]
    value_width = w_value.shape[2]
    rotary_width = q_rope.shape[1] // head_count
    block_size = latent_keys.shape[1]
    key_width = latent_keys.shape[2]
    score_scale = (nope_width + rotary_width) ** (-0.5)
    queries = q_nope.reshape(request_count, stretch_size, head_count, nope_width)
    absorbed = jnp.einsum(
        "kihd,hcd->kihc", queries, w_key, preferred_element_type=jnp.float32
    ).astype(jnp.bfloat16)
    rotary = q_rope.reshape(request_count, stretch_size, head_count, rotary_width)
    full_query = jnp.concatenate([absorbed, rotary], axis=3)
    query_pos = prefix_len[:, None] + jnp.arange(stretch_size, dtype=jnp.int32)[None, :]
    key_piece = lax.all_gather(latent_keys, "tensor", axis=1, tiled=True)
    running_max = jnp.full((request_count, stretch_size, head_count), -1e30, jnp.float32)
    scores = (
        jnp.einsum("kihc,kjc->kihj", full_query, key_piece, preferred_element_type=jnp.float32)
        * score_scale
    )
    key_pos = jnp.arange(key_piece.shape[1], dtype=jnp.int32)
    visible = key_pos[None, None, :] <= query_pos[:, :, None]
    scores = jnp.where(visible[:, :, None, :], scores, -1e30)
    new_max = jnp.maximum(running_max, jnp.max(scores, axis=3))
    weights = jnp.exp(scores - new_max[:, :, :, None])
    denom_sum = jnp.sum(weights, axis=3)
    added = jnp.einsum(
        "kihj,kjc->kihc",
        weights.astype(jnp.bfloat16),
        key_piece[:, :, :latent_width],
        preferred_element_type=jnp.float32,
    )
    accum = added
    running_max, denom_sum, accum = (new_max, denom_sum, accum)
    latent_out = (accum / denom_sum[:, :, :, None]).astype(jnp.bfloat16)
    head_out = jnp.einsum(
        "kihc,hcv->kihv", latent_out, w_value, preferred_element_type=jnp.float32
    ).astype(jnp.bfloat16)
    live_rows = jnp.arange(stretch_size, dtype=jnp.int32)[None, :] < stretch_len[:, None]
    head_out = jnp.where(live_rows[:, :, None, None], head_out, jnp.zeros_like(head_out))
    rank_count = lax.axis_size("request")
    tensor_count = lax.axis_size("tensor")
    share_rows = row_count // tensor_count
    head_rows = head_out.reshape(tensor_count, share_rows, head_count * value_width)
    all_rows = lax.all_gather(head_rows, "request", axis=1, tiled=True)
    terms = jnp.dot(
        all_rows.reshape(rank_count * row_count, head_count * value_width),
        w_out,
        preferred_element_type=jnp.float32,
    ).astype(jnp.bfloat16)
    summed = lax.psum_scatter(terms, "tensor", scatter_dimension=0, tiled=True)
    mixed = lax.all_to_all(
        summed.reshape(rank_count, share_rows, w_out.shape[1]),
        "request",
        split_axis=0,
        concat_axis=2,
        tiled=True,
    )
    block_index = lax.axis_index("tensor")
    seq_ends = prefix_len + stretch_len
    positions = block_index * block_size + jnp.arange(block_size, dtype=jnp.int32)
    live_keys = (positions[None, :] < seq_ends[:, None]) & (finished[:, None] > 0)
    kept = jnp.where(live_keys[:, :, None], latent_keys, jnp.zeros_like(latent_keys))
    owner_here = owners[:, 0]
    routing = (owner_here[:, None] == jnp.arange(rank_count, dtype=jnp.int32)[None, :]).astype(
        jnp.bfloat16
    )
    outgoing = jnp.einsum("ko,kjc->ojc", routing, kept, preferred_element_type=jnp.float32).astype(
        jnp.bfloat16
    )
    arrived = lax.all_to_all(outgoing, "request", split_axis=0, concat_axis=0, tiled=True)
    handed = arrived.reshape(1, rank_count, block_size, key_width)
    return (mixed, handed)


def solution(mesh):
    placed = (
        P(("groups", "request"), "tensor"),
        P(("groups", "request"), "tensor"),
        P(("groups", "request"), "tensor", None),
        P("tensor", None, None),
        P("tensor", None, None),
        P("tensor", "request"),
        P(("groups", "request")),
        P(("groups", "request")),
        P(("groups", "request")),
        P(("groups", "request"), "tensor"),
    )
    return jax.shard_map(
        local,
        mesh=mesh,
        in_specs=placed,
        out_specs=(
            P(("groups", "request"), "tensor", None),
            P(("groups", "request"), None, "tensor", None),
        ),
        check_vma=False,
    )
```

```python
import jax
import jax.numpy as jnp
from jax import lax
from jax.sharding import PartitionSpec as P


def swap(value, axis, distance, inner=1):
    size = lax.axis_size(axis)
    pairs = [(i, ((i // inner) ^ distance) * inner + i % inner) for i in range(size)]
    return lax.ppermute(value, axis, pairs)


def by_rank(pieces, rank):
    distance = 1
    while distance < len(pieces):
        flip = (rank & distance) > 0
        pieces = [jnp.where(flip, pieces[k ^ distance], pieces[k]) for k in range(len(pieces))]
        distance *= 2
    return pieces


def gather_ranks(value, axis):
    size = lax.axis_size(axis)
    pieces = {0: value}
    distance = size // 2
    while distance:
        for k in list(pieces):
            pieces[k ^ distance] = swap(pieces[k], axis, distance)
        distance //= 2
    return [pieces[k] for k in range(size)]


def local(
    q_nope, q_rope, latent_keys, w_key, w_value, w_out, prefix_len, stretch_len, finished, owners
):
    request_count = prefix_len.shape[0]
    row_count = q_nope.shape[0]
    stretch_size = row_count // request_count
    head_count = w_key.shape[0]
    latent_width = w_key.shape[1]
    nope_width = w_key.shape[2]
    value_width = w_value.shape[2]
    rotary_width = q_rope.shape[1] // head_count
    block_size = latent_keys.shape[1]
    key_width = latent_keys.shape[2]
    score_scale = (nope_width + rotary_width) ** (-0.5)
    rank_count = lax.axis_size("request")
    tensor_count = lax.axis_size("tensor")
    inner = tensor_count // request_count
    share_rows = row_count // tensor_count
    rank = lax.axis_index("request")
    place = lax.axis_index("tensor")
    outer_place = place // inner

    seq_ends = prefix_len + stretch_len
    positions = place * block_size + jnp.arange(block_size, dtype=jnp.int32)
    live_keys = (positions[None, :] < seq_ends[:, None]) & (finished[:, None] > 0)
    kept = jnp.where(live_keys[:, :, None], latent_keys, jnp.zeros_like(latent_keys))
    targets = rank ^ jnp.arange(rank_count, dtype=jnp.int32)
    routing = (owners[:, :1] == targets[None, :]).astype(jnp.bfloat16)
    outgoing = jnp.einsum("ko,kjc->ojc", routing, kept, preferred_element_type=jnp.float32).astype(
        jnp.bfloat16
    )
    arrived = [outgoing[0]] + [swap(outgoing[k], "request", k) for k in range(1, rank_count)]
    handed = jnp.stack(by_rank(arrived, rank))[None]

    if inner > 1:
        groups = [[o * inner + i for i in range(inner)] for o in range(request_count)]
        own_keys = lax.all_gather(
            latent_keys, "tensor", axis=1, tiled=True, axis_index_groups=groups
        )
    else:
        own_keys = latent_keys
    near = (outer_place // 2) * 2
    far = near ^ 2
    near_keys = lax.dynamic_slice_in_dim(own_keys, near, 2, 0)
    far_keys = lax.dynamic_slice_in_dim(own_keys, far, 2, 0)
    far_two = swap(near_keys, "tensor", 2, inner)
    far_one = swap(far_keys, "tensor", 1, inner)
    far_three = swap(far_two, "tensor", 1, inner)
    near_two = swap(far_keys, "tensor", 2, inner)
    near_one = swap(near_keys, "tensor", 1, inner)
    near_three = swap(near_two, "tensor", 1, inner)
    far_blocks = [far_keys, far_one, far_two, far_three]
    near_blocks = [near_keys, near_one, near_two, near_three]

    queries = q_nope.reshape(row_count, head_count, nope_width)
    absorbed = jnp.einsum(
        "ihd,hcd->hic", queries, w_key, preferred_element_type=jnp.float32
    ).astype(jnp.bfloat16)
    rotary = q_rope.reshape(row_count, head_count, rotary_width).transpose(1, 0, 2)
    full_query = jnp.concatenate([absorbed, rotary], axis=2)
    span = own_keys.shape[1]
    key_pos = jnp.concatenate(
        [(outer_place ^ k) * span + jnp.arange(span, dtype=jnp.int32) for k in range(4)]
    )

    def stage(distance):
        request = outer_place ^ distance
        blocks = far_blocks if distance >= 2 else near_blocks
        keys = jnp.concatenate(
            [lax.dynamic_index_in_dim(b, request % 2, 0, False) for b in blocks], axis=0
        )
        query = lax.dynamic_slice_in_dim(full_query, request * stretch_size, stretch_size, 1)
        scores = (
            jnp.einsum("hic,jc->hij", query, keys, preferred_element_type=jnp.float32)
            * score_scale
        )
        query_pos = prefix_len[request] + jnp.arange(stretch_size, dtype=jnp.int32)
        visible = key_pos[None, :] <= query_pos[:, None]
        scores = jnp.where(visible[None], scores, -1e30)
        weights = jnp.exp(scores - jnp.max(scores, axis=2, keepdims=True))
        denom = jnp.sum(weights, axis=2, keepdims=True)
        added = jnp.einsum(
            "hij,jc->hic",
            weights.astype(jnp.bfloat16),
            keys[:, :latent_width],
            preferred_element_type=jnp.float32,
        )
        latent_out = (added / denom).astype(jnp.bfloat16)
        head_out = jnp.einsum(
            "hic,hcv->ihv", latent_out, w_value, preferred_element_type=jnp.float32
        ).astype(jnp.bfloat16)
        live = jnp.arange(stretch_size, dtype=jnp.int32) < stretch_len[request]
        head_out = jnp.where(live[:, None, None], head_out, jnp.zeros_like(head_out))
        head_rows = head_out.reshape(stretch_size, head_count * value_width)
        rows = jnp.stack(gather_ranks(head_rows, "request"))
        return jnp.dot(
            rows.reshape(rank_count * stretch_size, head_count * value_width),
            w_out,
            preferred_element_type=jnp.float32,
        )

    opposite = swap(stage(3).astype(jnp.bfloat16), "tensor", 1, inner)
    across = swap((stage(2) + opposite).astype(jnp.bfloat16), "tensor", 2, inner)
    beside = swap(stage(1).astype(jnp.bfloat16), "tensor", 1, inner)
    summed = (stage(0) + beside + across).astype(jnp.bfloat16)
    if inner > 1:
        summed = summed.reshape(rank_count, inner, share_rows, summed.shape[1]).swapaxes(0, 1)
        summed = lax.psum_scatter(
            summed, "tensor", scatter_dimension=0, axis_index_groups=groups, tiled=True
        )
    summed = summed.reshape(rank_count, share_rows, w_out.shape[1])
    columns = [summed[0]] + [swap(summed[k], "request", k) for k in range(1, rank_count)]
    mixed = jnp.concatenate(by_rank(columns, rank), axis=1)[None]
    return (mixed, handed)


def solution(mesh):
    placed = (
        P(("groups", "request"), "tensor"),
        P(("groups", "request"), "tensor"),
        P(("groups", "request"), "tensor", None),
        P("tensor", None, None),
        P("tensor", None, None),
        P("tensor", "request"),
        P(("groups", "request")),
        P(("groups", "request")),
        P(("groups", "request")),
        P(("groups", "request"), "tensor"),
    )
    return jax.shard_map(
        local,
        mesh=mesh,
        in_specs=placed,
        out_specs=(
            P(("groups", "request"), "tensor", None),
            P(("groups", "request"), None, "tensor", None),
        ),
        check_vma=False,
    )
```

```python
import functools
import math

import jax
import jax.numpy as jnp
from jax import lax
from jax.experimental import pallas as pl
from jax.experimental.pallas import tpu as pltpu
from jax.sharding import PartitionSpec as P

MIB = 1 << 20


def swap(value, axis, distance, inner=1):
    size = lax.axis_size(axis)
    pairs = [(i, ((i // inner) ^ distance) * inner + i % inner) for i in range(size)]
    return lax.ppermute(value, axis, pairs)


def by_rank(pieces, rank):
    distance = 1
    while distance < len(pieces):
        flip = (rank & distance) > 0
        pieces = [jnp.where(flip, pieces[k ^ distance], pieces[k]) for k in range(len(pieces))]
        distance *= 2
    return pieces


def gather_ranks(value, axis):
    size = lax.axis_size(axis)
    pieces = {0: value}
    distance = size // 2
    while distance:
        for k in list(pieces):
            pieces[k ^ distance] = swap(pieces[k], axis, distance)
        distance //= 2
    return [pieces[k] for k in range(size)]


def part_of(size, wanted, unit=1):
    return max(d for d in range(unit, max(wanted, unit) + 1, unit) if size % d == 0)


def absorb_kernel(nope_ref, rope_ref, key_ref, out_ref):
    heads, latent, nope = key_ref.shape
    rotary = out_ref.shape[2] - latent
    for h in range(heads):
        out_ref[h, :, :latent] = lax.dot_general(
            nope_ref[:, h * nope : (h + 1) * nope],
            key_ref[h],
            (((1,), (1,)), ((), ())),
            preferred_element_type=jnp.float32,
        ).astype(out_ref.dtype)
        out_ref[h, :, latent:] = rope_ref[:, h * rotary : (h + 1) * rotary]


def absorb(q_nope, q_rope, w_key):
    rows = q_nope.shape[0]
    heads, latent, nope = w_key.shape
    rotary = q_rope.shape[1] // heads
    step = part_of(heads, 4, 2)
    return pl.pallas_call(
        absorb_kernel,
        grid=(heads // step,),
        in_specs=[
            pl.BlockSpec((rows, step * nope), lambda h: (0, h)),
            pl.BlockSpec((rows, step * rotary), lambda h: (0, h)),
            pl.BlockSpec((step, latent, nope), lambda h: (h, 0, 0)),
        ],
        out_specs=pl.BlockSpec((step, rows, latent + rotary), lambda h: (h, 0, 0)),
        out_shape=jax.ShapeDtypeStruct((heads, rows, latent + rotary), q_nope.dtype),
        compiler_params=pltpu.CompilerParams(vmem_limit_bytes=24 * MIB),
        cost_estimate=pl.CostEstimate(
            flops=2 * rows * heads * latent * nope,
            bytes_accessed=2 * (q_nope.size + q_rope.size + w_key.size)
            + 2 * heads * rows * (latent + rotary),
            transcendentals=0,
        ),
        name="absorb",
    )(q_nope, q_rope, w_key)


def attend_kernel(
    distance, scale, place_ref, prefix_ref, stretch_ref, query_ref, *refs
):
    block_refs, (value_ref, out_ref, keys, hidden) = refs[:4], refs[4:]
    heads, stretch, width = query_ref.shape
    latent, value_width = value_ref.shape[1:]
    part = block_refs[0].shape[1]
    span = 4 * part
    place = place_ref[0]
    request = place ^ distance

    @pl.when(pl.program_id(0) == 0)
    def _():
        query_pos = prefix_ref[request] + lax.broadcasted_iota(jnp.int32, (stretch, part), 0)
        for k, ref in enumerate(block_refs):
            keys[k * part : (k + 1) * part] = ref[0]
            key_pos = (place ^ k) * part + lax.broadcasted_iota(jnp.int32, (stretch, part), 1)
            hidden[:, k * part : (k + 1) * part] = jnp.where(key_pos <= query_pos, 0.0, -1e30)

    query = query_ref[...].reshape(heads * stretch, width)
    scores = lax.dot_general(
        query, keys[...], (((1,), (1,)), ((), ())), preferred_element_type=jnp.float32
    )
    scores = scores.reshape(heads, stretch, span) + hidden[...][None]
    top = jnp.max(scores, axis=2, keepdims=True)
    weights = jnp.exp2((scores - top) * (scale / math.log(2.0)))
    denom = jnp.sum(weights, axis=2, keepdims=True).reshape(heads * stretch, 1)
    latent_out = jnp.dot(
        weights.astype(jnp.bfloat16).reshape(heads * stretch, span),
        keys[:, :latent],
        preferred_element_type=jnp.float32,
    )
    latent_out = (latent_out / denom).astype(jnp.bfloat16)
    live = lax.broadcasted_iota(jnp.int32, (stretch, value_width), 0) < stretch_ref[request]
    for h in range(heads):
        head_out = jnp.dot(
            latent_out[h * stretch : (h + 1) * stretch],
            value_ref[h],
            preferred_element_type=jnp.float32,
        )
        out_ref[:, h * value_width : (h + 1) * value_width] = jnp.where(
            live, head_out, 0.0
        ).astype(out_ref.dtype)


def attend(distance, place, prefix_len, stretch_len, full_query, blocks, w_value, scale):
    heads, rows, width = full_query.shape
    latent, value_width = w_value.shape[1:]
    stretch = rows // prefix_len.shape[0]
    part = blocks[0].shape[1]
    step = part_of(heads, 8)
    span = 4 * part
    return pl.pallas_call(
        functools.partial(attend_kernel, distance, scale),
        grid_spec=pltpu.PrefetchScalarGridSpec(
            num_scalar_prefetch=3,
            grid=(heads // step,),
            in_specs=[
                pl.BlockSpec((step, stretch, width), lambda h, p, *_: (h, p[0] ^ distance, 0))
            ]
            + [pl.BlockSpec((1, part, width), lambda h, p, *_: ((p[0] ^ distance) % 2, 0, 0))] * 4
            + [pl.BlockSpec((step, latent, value_width), lambda h, *_: (h, 0, 0))],
            out_specs=pl.BlockSpec((stretch, step * value_width), lambda h, *_: (0, h)),
            scratch_shapes=[
                pltpu.VMEM((span, width), jnp.bfloat16),
                pltpu.VMEM((stretch, span), jnp.float32),
            ],
        ),
        out_shape=jax.ShapeDtypeStruct((stretch, heads * value_width), jnp.bfloat16),
        compiler_params=pltpu.CompilerParams(vmem_limit_bytes=32 * MIB),
        cost_estimate=pl.CostEstimate(
            flops=2 * stretch * heads * (span * (width + latent) + latent * value_width),
            bytes_accessed=2 * (heads * stretch * (width + value_width) + span * width + w_value.size),
            transcendentals=stretch * heads * span,
        ),
        name=f"attend_{distance}",
    )(place, prefix_len, stretch_len, full_query, *blocks, w_value)


def project_kernel(rank_count, has_extra, *refs):
    row_refs, refs = refs[:rank_count], refs[rank_count:]
    weight_ref, refs = refs[0], refs[1:]
    extra_refs, (out_ref, rows) = refs[:-2], refs[-2:]
    stretch = row_refs[0].shape[0]

    @pl.when(pl.program_id(0) == 0)
    def _():
        for k, ref in enumerate(row_refs):
            rows[k * stretch : (k + 1) * stretch] = ref[...]

    total = jnp.dot(rows[...], weight_ref[...], preferred_element_type=jnp.float32)
    for ref in extra_refs:
        total += ref[...].astype(jnp.float32)
    out_ref[...] = total.astype(out_ref.dtype)


def project(pieces, w_out, extras, dtype, name):
    stretch, depth = pieces[0].shape
    columns = w_out.shape[1]
    rows = stretch * len(pieces)
    step = part_of(columns, 256, 128)
    return pl.pallas_call(
        functools.partial(project_kernel, len(pieces), len(extras)),
        grid=(columns // step,),
        in_specs=[pl.BlockSpec((stretch, depth), lambda n: (0, 0))] * len(pieces)
        + [pl.BlockSpec((depth, step), lambda n: (0, n))]
        + [pl.BlockSpec((rows, step), lambda n: (0, n))] * len(extras),
        out_specs=pl.BlockSpec((rows, step), lambda n: (0, n)),
        out_shape=jax.ShapeDtypeStruct((rows, columns), dtype),
        scratch_shapes=[pltpu.VMEM((rows, depth), jnp.bfloat16)],
        compiler_params=pltpu.CompilerParams(vmem_limit_bytes=32 * MIB),
        cost_estimate=pl.CostEstimate(
            flops=2 * rows * depth * columns,
            bytes_accessed=2 * (rows * depth + w_out.size + rows * columns * (1 + len(extras))),
            transcendentals=0,
        ),
        name=name,
    )(*pieces, w_out, *extras)


def local(
    q_nope, q_rope, latent_keys, w_key, w_value, w_out, prefix_len, stretch_len, finished, owners
):
    request_count = prefix_len.shape[0]
    row_count = q_nope.shape[0]
    head_count, latent_width, nope_width = w_key.shape
    rotary_width = q_rope.shape[1] // head_count
    block_size = latent_keys.shape[1]
    score_scale = (nope_width + rotary_width) ** (-0.5)
    rank_count = lax.axis_size("request")
    tensor_count = lax.axis_size("tensor")
    inner = tensor_count // request_count
    share_rows = row_count // tensor_count
    rank = lax.axis_index("request")
    place = lax.axis_index("tensor")
    outer_place = place // inner

    if inner > 1:
        groups = [[o * inner + i for i in range(inner)] for o in range(request_count)]
        own_keys = lax.all_gather(
            latent_keys, "tensor", axis=1, tiled=True, axis_index_groups=groups
        )
    else:
        own_keys = latent_keys
    near = (outer_place // 2) * 2
    near_keys = lax.dynamic_slice_in_dim(own_keys, near, 2, 0)
    far_keys = lax.dynamic_slice_in_dim(own_keys, near ^ 2, 2, 0)
    far_two = swap(near_keys, "tensor", 2, inner)
    far_one = swap(far_keys, "tensor", 1, inner)
    far_three = swap(far_two, "tensor", 1, inner)
    near_two = swap(far_keys, "tensor", 2, inner)
    near_one = swap(near_keys, "tensor", 1, inner)
    near_three = swap(near_two, "tensor", 1, inner)
    far_blocks = [far_keys, far_one, far_two, far_three]
    near_blocks = [near_keys, near_one, near_two, near_three]

    seq_ends = prefix_len + stretch_len
    positions = place * block_size + jnp.arange(block_size, dtype=jnp.int32)
    live_keys = (positions[None, :] < seq_ends[:, None]) & (finished[:, None] > 0)
    kept = jnp.where(live_keys[:, :, None], latent_keys, jnp.zeros_like(latent_keys))
    targets = rank ^ jnp.arange(rank_count, dtype=jnp.int32)
    routing = (owners[:, :1] == targets[None, :]).astype(jnp.bfloat16)
    outgoing = jnp.einsum("ko,kjc->ojc", routing, kept, preferred_element_type=jnp.float32).astype(
        jnp.bfloat16
    )
    arrived = [outgoing[0]] + [swap(outgoing[k], "request", k) for k in range(1, rank_count)]
    handed = jnp.stack(by_rank(arrived, rank))[None]

    full_query = absorb(q_nope, q_rope, w_key)
    place_here = outer_place.reshape(1)

    def rows_of(distance):
        blocks = far_blocks if distance >= 2 else near_blocks
        head_rows = attend(
            distance,
            place_here,
            prefix_len,
            stretch_len,
            full_query,
            blocks,
            w_value,
            score_scale,
        )
        return gather_ranks(head_rows, "request")

    sent = jnp.bfloat16
    opposite = swap(project(rows_of(3), w_out, [], sent, "project_3"), "tensor", 1, inner)
    across = swap(project(rows_of(2), w_out, [opposite], sent, "project_2"), "tensor", 2, inner)
    beside = swap(project(rows_of(1), w_out, [], sent, "project_1"), "tensor", 1, inner)
    kept_terms = project(rows_of(0), w_out, [], jnp.float32, "project_0")
    summed = (kept_terms + beside + across).astype(sent)
    if inner > 1:
        summed = summed.reshape(rank_count, inner, share_rows, summed.shape[1]).swapaxes(0, 1)
        summed = lax.psum_scatter(
            summed, "tensor", scatter_dimension=0, axis_index_groups=groups, tiled=True
        )
    summed = summed.reshape(rank_count, share_rows, w_out.shape[1])
    columns = [summed[0]] + [swap(summed[k], "request", k) for k in range(1, rank_count)]
    mixed = jnp.concatenate(by_rank(columns, rank), axis=1)[None]
    return (mixed, handed)


def solution(mesh):
    placed = (
        P(("groups", "request"), "tensor"),
        P(("groups", "request"), "tensor"),
        P(("groups", "request"), "tensor", None),
        P("tensor", None, None),
        P("tensor", None, None),
        P("tensor", "request"),
        P(("groups", "request")),
        P(("groups", "request")),
        P(("groups", "request")),
        P(("groups", "request"), "tensor"),
    )
    return jax.shard_map(
        local,
        mesh=mesh,
        in_specs=placed,
        out_specs=(
            P(("groups", "request"), "tensor", None),
            P(("groups", "request"), None, "tensor", None),
        ),
        check_vma=False,
    )
```

```python
import functools
import math

import jax
import jax.numpy as jnp
from jax import lax
from jax.experimental import pallas as pl
from jax.experimental.pallas import tpu as pltpu
from jax.sharding import PartitionSpec as P

MIB = 1 << 20


def swap(value, axis, distance, inner=1):
    size = lax.axis_size(axis)
    pairs = [(i, ((i // inner) ^ distance) * inner + i % inner) for i in range(size)]
    return lax.ppermute(value, axis, pairs)


def after(value, *others):
    return lax.optimization_barrier((value, *others))[0]


def gather_ranks(value, axis, *earlier):
    size = lax.axis_size(axis)
    pieces = {0: value}
    distance = size // 2
    while distance:
        for k in list(pieces):
            passed = after(pieces[k], *earlier) if k and earlier else pieces[k]
            pieces[k ^ distance] = swap(passed, axis, distance)
        distance //= 2
    return [pieces[k] for k in range(size)]


def part_of(size, wanted, unit=1):
    return max(d for d in range(unit, max(wanted, unit) + 1, unit) if size % d == 0)


def split_columns(width):
    unit = 256 if width % 256 == 0 else 128
    first = width // unit // 2 * unit
    return [(0, first), (first, width - first)] if width % 256 == 0 and first else [(0, width)]


def absorb_kernel(nope_ref, rope_ref, key_ref, out_ref):
    heads, latent, nope = key_ref.shape
    rotary = out_ref.shape[2] - latent
    for h in range(heads):
        out_ref[h, :, :latent] = lax.dot_general(
            nope_ref[:, h * nope : (h + 1) * nope],
            key_ref[h],
            (((1,), (1,)), ((), ())),
            preferred_element_type=jnp.float32,
        ).astype(out_ref.dtype)
        out_ref[h, :, latent:] = rope_ref[:, h * rotary : (h + 1) * rotary]


def absorb(q_nope, q_rope, w_key):
    rows = q_nope.shape[0]
    heads, latent, nope = w_key.shape
    rotary = q_rope.shape[1] // heads
    step = part_of(heads, 4, 2)
    return pl.pallas_call(
        absorb_kernel,
        grid=(heads // step,),
        in_specs=[
            pl.BlockSpec((rows, step * nope), lambda h: (0, h)),
            pl.BlockSpec((rows, step * rotary), lambda h: (0, h)),
            pl.BlockSpec((step, latent, nope), lambda h: (h, 0, 0)),
        ],
        out_specs=pl.BlockSpec((step, rows, latent + rotary), lambda h: (h, 0, 0)),
        out_shape=jax.ShapeDtypeStruct((heads, rows, latent + rotary), q_nope.dtype),
        compiler_params=pltpu.CompilerParams(vmem_limit_bytes=8 * MIB),
        cost_estimate=pl.CostEstimate(flops=1, bytes_accessed=1, transcendentals=0),
        name="absorb",
    )(q_nope, q_rope, w_key)


def attend_kernel(
    distance, scale, ids_ref, prefix_ref, stretch_ref, query_ref, *refs
):
    block_refs, (value_ref, out_ref, keys, hidden) = refs[:4], refs[4:]
    heads, stretch, width = query_ref.shape
    latent, value_width = value_ref.shape[1:]
    part = block_refs[0].shape[2]
    span = 4 * part
    place = ids_ref[0]
    request = place ^ distance

    @pl.when(pl.program_id(0) == 0)
    def _():
        query_pos = prefix_ref[request] + lax.broadcasted_iota(jnp.int32, (stretch, part), 0)
        for k, ref in enumerate(block_refs):
            keys[:, k * part : (k + 1) * part] = ref[0]
            key_pos = (place ^ k) * part + lax.broadcasted_iota(jnp.int32, (stretch, part), 1)
            hidden[:, k * part : (k + 1) * part] = jnp.where(key_pos <= query_pos, 0.0, -1e30)

    query = query_ref[...].reshape(heads * stretch, width)
    scores = jnp.dot(query, keys[...], preferred_element_type=jnp.float32)
    scores = scores.reshape(heads, stretch, span) + hidden[...][None]
    top = jnp.max(scores, axis=2, keepdims=True)
    weights = jnp.exp2((scores - top) * (scale / math.log(2.0)))
    denom = jnp.sum(weights, axis=2, keepdims=True).reshape(heads * stretch, 1)
    latent_out = lax.dot_general(
        weights.astype(jnp.bfloat16).reshape(heads * stretch, span),
        keys[:latent],
        (((1,), (1,)), ((), ())),
        preferred_element_type=jnp.float32,
    )
    latent_out = (latent_out / denom).astype(jnp.bfloat16)
    live = lax.broadcasted_iota(jnp.int32, (stretch, value_width), 0) < stretch_ref[request]
    for h in range(heads):
        head_out = jnp.dot(
            latent_out[h * stretch : (h + 1) * stretch],
            value_ref[h],
            preferred_element_type=jnp.float32,
        )
        out_ref[:, h * value_width : (h + 1) * value_width] = jnp.where(
            live, head_out, 0.0
        ).astype(out_ref.dtype)


def attend(distance, ids, prefix_len, stretch_len, full_query, blocks, w_value, scale):
    heads, rows, width = full_query.shape
    latent, value_width = w_value.shape[1:]
    stretch = rows // prefix_len.shape[0]
    part = blocks[0].shape[2]
    step = part_of(heads, 8)
    span = 4 * part
    return pl.pallas_call(
        functools.partial(attend_kernel, distance, scale),
        grid_spec=pltpu.PrefetchScalarGridSpec(
            num_scalar_prefetch=3,
            grid=(heads // step,),
            in_specs=[
                pl.BlockSpec((step, stretch, width), lambda h, p, *_: (h, p[0] ^ distance, 0))
            ]
            + [pl.BlockSpec((1, width, part), lambda h, p, *_: ((p[0] ^ distance) % 2, 0, 0))] * 4
            + [pl.BlockSpec((step, latent, value_width), lambda h, *_: (h, 0, 0))],
            out_specs=pl.BlockSpec((stretch, step * value_width), lambda h, *_: (0, h)),
            scratch_shapes=[
                pltpu.VMEM((width, span), jnp.bfloat16),
                pltpu.VMEM((stretch, span), jnp.float32),
            ],
        ),
        out_shape=jax.ShapeDtypeStruct((stretch, heads * value_width), jnp.bfloat16),
        compiler_params=pltpu.CompilerParams(vmem_limit_bytes=10 * MIB * max(span // 512, 1)),
        cost_estimate=pl.CostEstimate(flops=1, bytes_accessed=1, transcendentals=0),
        name=f"attend_{distance}",
    )(ids, prefix_len, stretch_len, full_query, *blocks, w_value)


def project_kernel(rank_count, *refs):
    row_refs, (weight_ref, out_ref, rows) = refs[:rank_count], refs[rank_count:]
    stretch = row_refs[0].shape[0]

    @pl.when(pl.program_id(0) == 0)
    def _():
        for k, ref in enumerate(row_refs):
            rows[k * stretch : (k + 1) * stretch] = ref[...]

    total = jnp.dot(rows[...], weight_ref[...], preferred_element_type=jnp.float32)
    out_ref[...] = total.astype(out_ref.dtype)


def project(pieces, w_out, start, columns, dtype, name):
    stretch, depth = pieces[0].shape
    rows = stretch * len(pieces)
    step = part_of(math.gcd(start, columns), 256, 128)
    first = start // step
    return pl.pallas_call(
        functools.partial(project_kernel, len(pieces)),
        grid=(columns // step,),
        in_specs=[pl.BlockSpec((stretch, depth), lambda n: (0, 0))] * len(pieces)
        + [pl.BlockSpec((depth, step), lambda n: (0, first + n))],
        out_specs=pl.BlockSpec((rows, step), lambda n: (0, n)),
        out_shape=jax.ShapeDtypeStruct((rows, columns), dtype),
        scratch_shapes=[pltpu.VMEM((rows, depth), jnp.bfloat16)],
        compiler_params=pltpu.CompilerParams(vmem_limit_bytes=14 * MIB),
        cost_estimate=pl.CostEstimate(flops=1, bytes_accessed=1, transcendentals=0),
        name=name,
    )(*pieces, w_out)


SCALARS = pl.BlockSpec(memory_space=pltpu.SMEM)
WHOLE = pl.BlockSpec(memory_space=pltpu.VMEM)


def handoff_kernel(ids_ref, prefix_ref, stretch_ref, finished_ref, owner_ref, keys_ref, *outs):
    requests, width, block = keys_ref.shape
    pos = ids_ref[2] * block + lax.broadcasted_iota(jnp.int32, (width, block), 1)
    for k, out in enumerate(outs):
        chosen = jnp.zeros((width, block), jnp.float32)
        for q in range(requests):
            here = (finished_ref[q] > 0) & (owner_ref[q] == (ids_ref[1] ^ k))
            end = jnp.where(here, prefix_ref[q] + stretch_ref[q], 0)
            chosen = jnp.where(pos < end, keys_ref[q].astype(jnp.float32), chosen)
        out[...] = chosen.astype(out.dtype)


def handoff(ids, prefix_len, stretch_len, finished, owners, keys, rank_count):
    return pl.pallas_call(
        handoff_kernel,
        in_specs=[SCALARS] * 5 + [WHOLE],
        out_specs=[WHOLE] * rank_count,
        out_shape=[jax.ShapeDtypeStruct(keys.shape[1:], keys.dtype)] * rank_count,
        compiler_params=pltpu.CompilerParams(vmem_limit_bytes=8 * MIB),
        name="handoff",
    )(ids, prefix_len, stretch_len, finished, owners, keys)


def place_blocks_kernel(ids_ref, *refs):
    out = refs[-1]
    for k, ref in enumerate(refs[:-1]):
        out[ids_ref[1] ^ k] = ref[...]


def place_blocks(ids, pieces):
    return pl.pallas_call(
        place_blocks_kernel,
        in_specs=[SCALARS] + [WHOLE] * len(pieces),
        out_specs=WHOLE,
        out_shape=jax.ShapeDtypeStruct((len(pieces), *pieces[0].shape), pieces[0].dtype),
        compiler_params=pltpu.CompilerParams(vmem_limit_bytes=8 * MIB),
        name="place_blocks",
    )(ids, *pieces)


def place_columns_kernel(splits, ids_ref, *refs):
    out = refs[-1]
    width = sum(columns for _, columns in splits)
    for n, ref in enumerate(refs[:-1]):
        k, part = divmod(n, len(splits))
        start, columns = splits[part]
        start = pl.multiple_of((ids_ref[1] ^ k) * width + start, 128)
        out[:, pl.ds(start, columns)] = ref[...]


def place_columns(ids, pieces, splits):
    rows = pieces[0].shape[0]
    width = sum(piece.shape[1] for piece in pieces)
    return pl.pallas_call(
        functools.partial(place_columns_kernel, splits),
        in_specs=[SCALARS] + [WHOLE] * len(pieces),
        out_specs=WHOLE,
        out_shape=jax.ShapeDtypeStruct((rows, width), pieces[0].dtype),
        compiler_params=pltpu.CompilerParams(vmem_limit_bytes=8 * MIB),
        name="place_columns",
    )(ids, *pieces)


def local(
    q_nope, q_rope, latent_keys, w_key, w_value, w_out, prefix_len, stretch_len, finished, owners
):
    request_count = prefix_len.shape[0]
    row_count = q_nope.shape[0]
    head_count, latent_width, nope_width = w_key.shape
    rotary_width = q_rope.shape[1] // head_count
    score_scale = (nope_width + rotary_width) ** (-0.5)
    rank_count = lax.axis_size("request")
    tensor_count = lax.axis_size("tensor")
    inner = tensor_count // request_count
    share_rows = row_count // tensor_count
    rank = lax.axis_index("request")
    place = lax.axis_index("tensor")
    outer_place = place // inner
    ids = jnp.stack([outer_place, rank, place]).astype(jnp.int32)

    block_keys = latent_keys.transpose(0, 2, 1)
    if inner > 1:
        groups = [[o * inner + i for i in range(inner)] for o in range(request_count)]
        own_keys = lax.all_gather(
            block_keys, "tensor", axis=2, tiled=True, axis_index_groups=groups
        )
    else:
        own_keys = block_keys
    near = (outer_place // 2) * 2
    near_keys = lax.dynamic_slice_in_dim(own_keys, near, 2, 0)
    far_keys = lax.dynamic_slice_in_dim(own_keys, near ^ 2, 2, 0)
    far_two = swap(near_keys, "tensor", 2, inner)
    far_one = swap(far_keys, "tensor", 1, inner)

    outgoing = handoff(
        after(ids, far_keys, near_keys),
        prefix_len,
        stretch_len,
        finished,
        owners.reshape(request_count),
        block_keys,
        rank_count,
    )
    full_query = absorb(after(q_nope, *outgoing), q_rope, w_key)
    arrived = [outgoing[0]] + [
        swap(after(outgoing[k], full_query), "request", k) for k in range(1, rank_count)
    ]
    far_three = swap(after(far_two, full_query), "tensor", 1, inner)
    near_two = swap(after(far_keys, far_three), "tensor", 2, inner)
    near_one = swap(after(near_keys, far_three), "tensor", 1, inner)
    far_blocks = [far_keys, far_one, far_two, far_three]
    near_blocks = [near_keys, near_one, near_two]

    def rows_of(distance, blocks, *earlier):
        return attend(
            distance,
            after(ids, *earlier),
            prefix_len,
            stretch_len,
            full_query,
            blocks,
            w_value,
            score_scale,
        )

    splits = split_columns(w_out.shape[1])
    parts = len(splits)
    sent = jnp.bfloat16

    def terms_of(distance, pieces, dtype, *earlier):
        pieces = [after(pieces[0], *earlier)] + pieces[1:]
        return [
            project(pieces, w_out, start, columns, dtype, f"project_{distance}_{start}")
            for start, columns in splits
        ]

    rows_3 = rows_of(3, far_blocks, *arrived)
    rows_2 = rows_of(2, far_blocks, rows_3)
    pieces_3 = gather_ranks(rows_3, "request", rows_2, near_one, near_two)
    terms_3 = terms_of(3, pieces_3, sent, rows_2)
    opposite = [swap(t, "tensor", 1, inner) for t in terms_3]
    near_blocks.append(swap(near_two, "tensor", 1, inner))
    rows_1 = rows_of(1, near_blocks, *terms_3)
    handed = place_blocks(after(ids, rows_1), arrived)
    rows_0 = rows_of(0, near_blocks, rows_1, handed, opposite[-1])
    pieces_2 = gather_ranks(rows_2, "request")
    terms_2 = terms_of(2, pieces_2, jnp.float32, rows_0)
    sums = [(t + o).astype(sent) for t, o in zip(terms_2, opposite)]
    across = [swap(t, "tensor", 2, inner) for t in sums]
    pieces_1 = gather_ranks(rows_1, "request")
    terms_1 = terms_of(1, pieces_1, sent, *sums)
    beside = [swap(t, "tensor", 1, inner) for t in terms_1]
    pieces_0 = gather_ranks(rows_0, "request")
    terms_0 = terms_of(0, pieces_0, jnp.float32, across[-1], *terms_1)

    columns = {}
    earlier = terms_0
    for part in reversed(range(parts)):
        partial = after(terms_0[part] + beside[part], *earlier)
        summed = (partial + across[part]).astype(sent)
        if inner > 1:
            summed = summed.reshape(rank_count, inner, share_rows, summed.shape[1]).swapaxes(0, 1)
            summed = lax.psum_scatter(
                summed, "tensor", scatter_dimension=0, axis_index_groups=groups, tiled=True
            )
        summed = summed.reshape(rank_count, share_rows, summed.shape[-1])
        earlier = [swap(summed[k], "request", k) for k in range(1, rank_count)]
        columns[part] = [summed[0]] + earlier
    ordered = [columns[part][k] for k in range(rank_count) for part in range(parts)]
    mixed = place_columns(ids, ordered, splits)[None]
    handed = handed.transpose(0, 2, 1)[None]
    return (mixed, handed)


def solution(mesh):
    placed = (
        P(("groups", "request"), "tensor"),
        P(("groups", "request"), "tensor"),
        P(("groups", "request"), "tensor", None),
        P("tensor", None, None),
        P("tensor", None, None),
        P("tensor", "request"),
        P(("groups", "request")),
        P(("groups", "request")),
        P(("groups", "request")),
        P(("groups", "request"), "tensor"),
    )
    return jax.shard_map(
        local,
        mesh=mesh,
        in_specs=placed,
        out_specs=(
            P(("groups", "request"), "tensor", None),
            P(("groups", "request"), None, "tensor", None),
        ),
        check_vma=False,
    )
```

```python
import functools
import math

import jax
import jax.numpy as jnp
from jax import lax
from jax.experimental import pallas as pl
from jax.experimental.pallas import tpu as pltpu
from jax.sharding import PartitionSpec as P

MIB = 1 << 20
CFG = {'cost': 0.0, 'near': 'three', 'c': [3], 'b': [3], 'a': [3], 't': [3], 'h': [[4], [4], [4], [4]], 'arr': 3, 'p3r2': 1, 'p3n': 1, 'own3': 1, 't3r2': 1, 'cn': 1, 'cx2': 0, 'r0': 'post', 'core1': 'sums', 'own1': 0, 't1': 'sums', 'core0': 'first', 'own0': 1, 'hand': 'end', 't0': 'none', 'tail': [0, 1], 'tie': 1}


def cost(us):
    return pl.CostEstimate(
        flops=int(us * CFG["cost"] * 1.15e9) + 1, bytes_accessed=1, transcendentals=0
    )


def swap(value, axis, distance, inner=1):
    size = lax.axis_size(axis)
    pairs = [(i, ((i // inner) ^ distance) * inner + i % inner) for i in range(size)]
    return lax.ppermute(value, axis, pairs)


def after(value, *others):
    return lax.optimization_barrier((value, *others))[0]


def cross(values, axis):
    return [cross_one(value, axis) for value in values]


def spread(crossed, axis, *earlier, own=()):
    return [piece for pieces in crossed for piece in spread_one(pieces, axis, earlier, own)]


def cross_one(value, axis):
    pieces = {0: value}
    distance = lax.axis_size(axis) // 2
    while distance > 1:
        for k in list(pieces):
            pieces[k ^ distance] = swap(pieces[k], axis, distance)
        distance //= 2
    return pieces


def spread_one(pieces, axis, earlier, own):
    gates = {k: earlier if k else own for k in pieces}
    other = {k ^ 1: swap(after(v, *gates[k]), axis, 1) for k, v in pieces.items()}
    every = {**pieces, **other}
    return [every[k] for k in range(len(every))]


def part_of(size, wanted, unit=1):
    return max(d for d in range(unit, max(wanted, unit) + 1, unit) if size % d == 0)


def split_at(width, *places):
    edges = [0, *places, width]
    return [(a, b - a) for a, b in zip(edges, edges[1:]) if b > a]


def absorb_kernel(nope_ref, rope_ref, key_ref, out_ref):
    heads, latent, nope = key_ref.shape
    rotary = out_ref.shape[2] - latent
    for h in range(heads):
        out_ref[h, :, :latent] = lax.dot_general(
            nope_ref[:, h * nope : (h + 1) * nope],
            key_ref[h],
            (((1,), (1,)), ((), ())),
            preferred_element_type=jnp.float32,
        ).astype(out_ref.dtype)
        out_ref[h, :, latent:] = rope_ref[:, h * rotary : (h + 1) * rotary]


def absorb(q_nope, q_rope, w_key):
    rows = q_nope.shape[0]
    heads, latent, nope = w_key.shape
    rotary = q_rope.shape[1] // heads
    step = part_of(heads, 4, 2)
    return pl.pallas_call(
        absorb_kernel,
        grid=(heads // step,),
        in_specs=[
            pl.BlockSpec((rows, step * nope), lambda h: (0, h)),
            pl.BlockSpec((rows, step * rotary), lambda h: (0, h)),
            pl.BlockSpec((step, latent, nope), lambda h: (h, 0, 0)),
        ],
        out_specs=pl.BlockSpec((step, rows, latent + rotary), lambda h: (h, 0, 0)),
        out_shape=jax.ShapeDtypeStruct((heads, rows, latent + rotary), q_nope.dtype),
        compiler_params=pltpu.CompilerParams(vmem_limit_bytes=8 * MIB),
        cost_estimate=cost(3),
        name="absorb",
    )(q_nope, q_rope, w_key)


def attend_kernel(
    distance, scale, ids_ref, prefix_ref, stretch_ref, query_ref, *refs
):
    block_refs, value_ref, out_refs, (keys, hidden) = refs[:4], refs[4], refs[5:-2], refs[-2:]
    heads, stretch, width = query_ref.shape
    each = pl.num_programs(0) // len(out_refs)
    latent, value_width = value_ref.shape[1:]
    part = block_refs[0].shape[2]
    span = 4 * part
    place = ids_ref[0]
    request = place ^ distance

    @pl.when(pl.program_id(0) == 0)
    def _():
        query_pos = prefix_ref[request] + lax.broadcasted_iota(jnp.int32, (stretch, part), 0)
        for k, ref in enumerate(block_refs):
            keys[:, k * part : (k + 1) * part] = ref[0]
            key_pos = (place ^ k) * part + lax.broadcasted_iota(jnp.int32, (stretch, part), 1)
            hidden[:, k * part : (k + 1) * part] = jnp.where(key_pos <= query_pos, 0.0, -1e30)

    query = query_ref[...].reshape(heads * stretch, width)
    scores = jnp.dot(query, keys[...], preferred_element_type=jnp.float32)
    scores = scores.reshape(heads, stretch, span) + hidden[...][None]
    top = jnp.max(scores, axis=2, keepdims=True)
    weights = jnp.exp2((scores - top) * (scale / math.log(2.0)))
    denom = jnp.sum(weights, axis=2, keepdims=True).reshape(heads * stretch, 1)
    latent_out = lax.dot_general(
        weights.astype(jnp.bfloat16).reshape(heads * stretch, span),
        keys[:latent],
        (((1,), (1,)), ((), ())),
        preferred_element_type=jnp.float32,
    )
    latent_out = (latent_out / denom).astype(jnp.bfloat16)
    live = lax.broadcasted_iota(jnp.int32, (stretch, value_width), 0) < stretch_ref[request]
    head_outs = []
    for h in range(heads):
        head_out = jnp.dot(
            latent_out[h * stretch : (h + 1) * stretch],
            value_ref[h],
            preferred_element_type=jnp.float32,
        )
        head_outs.append(jnp.where(live, head_out, 0.0).astype(out_refs[0].dtype))
    for part, out_ref in enumerate(out_refs):

        @pl.when(pl.program_id(0) // each == part)
        def _(out_ref=out_ref):
            for h in range(heads):
                out_ref[:, h * value_width : (h + 1) * value_width] = head_outs[h]


def attend(
    distance, ids, prefix_len, stretch_len, full_query, blocks, w_value, scale, halves
):
    heads, rows, width = full_query.shape
    latent, value_width = w_value.shape[1:]
    stretch = rows // prefix_len.shape[0]
    part = blocks[0].shape[2]
    step = part_of(heads // halves, 8)
    each = heads // halves // step
    span = 4 * part

    def half_of(half):
        return lambda h, *_: (0, jnp.clip(h - half * each, 0, each - 1))

    return pl.pallas_call(
        functools.partial(attend_kernel, distance, scale),
        grid_spec=pltpu.PrefetchScalarGridSpec(
            num_scalar_prefetch=3,
            grid=(heads // step,),
            in_specs=[
                pl.BlockSpec((step, stretch, width), lambda h, p, *_: (h, p[0] ^ distance, 0))
            ]
            + [pl.BlockSpec((1, width, part), lambda h, p, *_: ((p[0] ^ distance) % 2, 0, 0))] * 4
            + [pl.BlockSpec((step, latent, value_width), lambda h, *_: (h, 0, 0))],
            out_specs=[
                pl.BlockSpec((stretch, step * value_width), half_of(half)) for half in range(halves)
            ],
            scratch_shapes=[
                pltpu.VMEM((width, span), jnp.bfloat16),
                pltpu.VMEM((stretch, span), jnp.float32),
            ],
        ),
        out_shape=[jax.ShapeDtypeStruct((stretch, heads // halves * value_width), jnp.bfloat16)]
        * halves,
        compiler_params=pltpu.CompilerParams(vmem_limit_bytes=10 * MIB * max(span // 512, 1)),
        cost_estimate=cost(5),
        name=f"attend_{distance}",
    )(ids, prefix_len, stretch_len, full_query, *blocks, w_value)


def project_kernel(stretch, splits, *refs):
    out_refs = refs[-1 - len(splits) : -1]
    weight_ref, rows = refs[-2 - len(splits)], refs[-1]
    row_refs = refs[: -2 - len(splits)]
    step = weight_ref.shape[1]
    n = pl.program_id(0)

    @pl.when(n == 0)
    def _():
        start = 0
        for ref in row_refs:
            line, column = start % rows.shape[0], start // rows.shape[0] * ref.shape[1]
            rows[line : line + stretch, column : column + ref.shape[1]] = ref[...]
            start += stretch

    total = jnp.dot(rows[...], weight_ref[...], preferred_element_type=jnp.float32)
    for (start, columns), out_ref in zip(splits, out_refs):

        @pl.when((n * step >= start) & (n * step < start + columns))
        def _(out_ref=out_ref):
            out_ref[...] = total.astype(out_ref.dtype)


def project(pieces, w_out, splits, dtype, name):
    stretch = pieces[0].shape[0]
    depth, width = w_out.shape
    rows = stretch * sum(piece.shape[1] for piece in pieces) // depth
    step = functools.reduce(math.gcd, [columns for _, columns in splits])
    step = part_of(step, 256, 128)

    def block_of(start, columns):
        last = columns // step - 1
        return lambda n: (0, jnp.clip(n - start // step, 0, last))

    return pl.pallas_call(
        functools.partial(project_kernel, stretch, splits),
        grid=(width // step,),
        in_specs=[pl.BlockSpec(piece.shape, lambda n: (0, 0)) for piece in pieces]
        + [pl.BlockSpec((depth, step), lambda n: (0, n))],
        out_specs=[pl.BlockSpec((rows, step), block_of(*split)) for split in splits],
        out_shape=[jax.ShapeDtypeStruct((rows, columns), dtype) for _, columns in splits],
        scratch_shapes=[pltpu.VMEM((rows, depth), jnp.bfloat16)],
        compiler_params=pltpu.CompilerParams(vmem_limit_bytes=14 * MIB),
        cost_estimate=cost(5.5),
        name=name,
    )(*pieces, w_out)


SCALARS = pl.BlockSpec(memory_space=pltpu.SMEM)
WHOLE = pl.BlockSpec(memory_space=pltpu.VMEM)


def handoff_kernel(ids_ref, prefix_ref, stretch_ref, finished_ref, owner_ref, keys_ref, *outs):
    requests, width, block = keys_ref.shape
    pos = ids_ref[2] * block + lax.broadcasted_iota(jnp.int32, (width, block), 1)
    for k, out in enumerate(outs):
        chosen = jnp.zeros((width, block), jnp.float32)
        for q in range(requests):
            here = (finished_ref[q] > 0) & (owner_ref[q] == (ids_ref[1] ^ k))
            end = jnp.where(here, prefix_ref[q] + stretch_ref[q], 0)
            chosen = jnp.where(pos < end, keys_ref[q].astype(jnp.float32), chosen)
        out[...] = chosen.astype(out.dtype)


def handoff(ids, prefix_len, stretch_len, finished, owners, keys, rank_count):
    return pl.pallas_call(
        handoff_kernel,
        in_specs=[SCALARS] * 5 + [WHOLE],
        out_specs=[WHOLE] * rank_count,
        out_shape=[jax.ShapeDtypeStruct(keys.shape[1:], keys.dtype)] * rank_count,
        compiler_params=pltpu.CompilerParams(vmem_limit_bytes=8 * MIB),
        name="handoff",
    )(ids, prefix_len, stretch_len, finished, owners, keys)


def place_blocks_kernel(ids_ref, *refs):
    out = refs[-1]
    for k, ref in enumerate(refs[:-1]):
        out[ids_ref[1] ^ k] = ref[...]


def place_blocks(ids, pieces):
    return pl.pallas_call(
        place_blocks_kernel,
        in_specs=[SCALARS] + [WHOLE] * len(pieces),
        out_specs=WHOLE,
        out_shape=jax.ShapeDtypeStruct((len(pieces), *pieces[0].shape), pieces[0].dtype),
        compiler_params=pltpu.CompilerParams(vmem_limit_bytes=8 * MIB),
        name="place_blocks",
    )(ids, *pieces)


def place_columns_kernel(splits, ids_ref, *refs):
    out = refs[-1]
    width = sum(columns for _, columns in splits)
    for n, ref in enumerate(refs[:-1]):
        k, part = divmod(n, len(splits))
        start, columns = splits[part]
        start = pl.multiple_of((ids_ref[1] ^ k) * width + start, 128)
        out[:, pl.ds(start, columns)] = ref[...]


def place_columns(ids, pieces, splits):
    rows = pieces[0].shape[0]
    width = sum(piece.shape[1] for piece in pieces)
    return pl.pallas_call(
        functools.partial(place_columns_kernel, splits),
        in_specs=[SCALARS] + [WHOLE] * len(pieces),
        out_specs=WHOLE,
        out_shape=jax.ShapeDtypeStruct((rows, width), pieces[0].dtype),
        compiler_params=pltpu.CompilerParams(vmem_limit_bytes=8 * MIB),
        name="place_columns",
    )(ids, *pieces)


def local(
    q_nope, q_rope, latent_keys, w_key, w_value, w_out, prefix_len, stretch_len, finished, owners
):
    request_count = prefix_len.shape[0]
    row_count = q_nope.shape[0]
    head_count, latent_width, nope_width = w_key.shape
    rotary_width = q_rope.shape[1] // head_count
    score_scale = (nope_width + rotary_width) ** (-0.5)
    rank_count = lax.axis_size("request")
    tensor_count = lax.axis_size("tensor")
    inner = tensor_count // request_count
    share_rows = row_count // tensor_count
    rank = lax.axis_index("request")
    place = lax.axis_index("tensor")
    outer_place = place // inner
    ids = jnp.stack([outer_place, rank, place]).astype(jnp.int32)

    block_keys = latent_keys.transpose(0, 2, 1)
    if inner > 1:
        groups = [[o * inner + i for i in range(inner)] for o in range(request_count)]
        own_keys = lax.all_gather(
            block_keys, "tensor", axis=2, tiled=True, axis_index_groups=groups
        )
    else:
        own_keys = block_keys
    near = (outer_place // 2) * 2
    near_keys = lax.dynamic_slice_in_dim(own_keys, near, 2, 0)
    far_keys = lax.dynamic_slice_in_dim(own_keys, near ^ 2, 2, 0)
    far_two = swap(near_keys, "tensor", 2, inner)
    far_one = swap(far_keys, "tensor", 1, inner)

    outgoing = handoff(
        after(ids, far_keys, near_keys),
        prefix_len,
        stretch_len,
        finished,
        owners.reshape(request_count),
        block_keys,
        rank_count,
    )
    full_query = absorb(after(q_nope, *outgoing), q_rope, w_key)
    arrived = [outgoing[0]] + [
        swap(after(outgoing[k], full_query), "request", k) for k in range(1, rank_count)
    ]
    far_three = swap(after(far_two, far_one, full_query), "tensor", 1, inner)
    near_gate = [far_three] if CFG["near"] == "three" else [far_two, far_one]
    near_two = swap(after(far_keys, *near_gate), "tensor", 2, inner)
    near_one = swap(after(near_keys, *near_gate), "tensor", 1, inner)
    far_blocks = [far_keys, far_one, far_two, far_three]
    near_blocks = [near_keys, near_one, near_two]

    halves = 2 if head_count % 2 == 0 else 1

    def rows_of(distance, blocks, *earlier):
        return attend(
            distance,
            after(ids, *earlier),
            prefix_len,
            stretch_len,
            full_query,
            blocks,
            w_value,
            score_scale,
            halves,
        )

    width = w_out.shape[1]
    split = {k: split_at(width, *[256 * p for p in CFG[k]]) if width == 1792 else [(0, width)] for k in "cbat"}
    heads = [split_at(head_count, *[head_count * p // 8 for p in CFG["h"][k]]) for k in range(4)]
    sent = jnp.bfloat16

    def regroup(arrays, splits):
        if [x.shape[1] for x in arrays] == [size for _, size in splits]:
            return arrays
        whole = jnp.concatenate(arrays, axis=1) if len(arrays) > 1 else arrays[0]
        return [whole[:, start : start + size] for start, size in splits]

    def terms_of(distance, pieces, dtype, splits, *earlier):
        pieces = [after(pieces[0], *earlier)] + pieces[1:]
        return project(pieces, w_out, splits, dtype, f"project_{distance}")

    rows_3 = rows_of(3, far_blocks, heads[3], *(arrived if CFG["arr"] == 3 else []))
    cross_3 = cross(rows_3, "request")
    rows_2 = rows_of(2, far_blocks, heads[2], *rows_3, *(arrived if CFG["arr"] == 2 else []))
    cross_2 = cross(rows_2, "request")
    crossed_2 = [piece for pieces in cross_2 for k, piece in pieces.items() if k]
    gate = [*(rows_2 if CFG["p3r2"] else []), *([near_one, near_two] if CFG["p3n"] else [])]
    pieces_3 = spread(cross_3, "request", *gate, own=rows_2 if CFG["own3"] else ())
    terms_3 = terms_of(3, pieces_3, sent, split["c"], *(rows_2 if CFG["t3r2"] else []))
    near_blocks.append(swap(near_two, "tensor", 1, inner))
    gate = [*([near_blocks[3]] if CFG["cn"] else []), *(crossed_2 if CFG["cx2"] else [])]
    opposite = [swap(after(t, *gate), "tensor", 1, inner) for t in terms_3]
    rows_1 = rows_of(1, near_blocks, heads[1], *terms_3)
    cross_1 = cross(rows_1, "request")
    if CFG["r0"] != "post":
        rows_0 = rows_of(0, near_blocks, heads[0], *rows_1)
    pieces_2 = spread(cross_2, "request")
    terms_2 = terms_of(2, pieces_2, jnp.float32, split["b"], *(rows_0 if CFG["r0"] == "pre" else rows_1))
    sums = [(t + o).astype(sent) for t, o in zip(terms_2, regroup(opposite, split["b"]))]
    across = [swap(t, "tensor", 2, inner) for t in sums]
    if CFG["r0"] == "post":
        rows_0 = rows_of(0, near_blocks, heads[0], *sums)
    cross_0 = cross(rows_0, "request")
    gates = {"none": [], "sums": sums, "first": across[:1], "last": across[-1:]}
    pieces_1 = spread(cross_1, "request", *gates[CFG["core1"]], own=sums if CFG["own1"] else ())
    terms_1 = terms_of(1, pieces_1, sent, split["a"], *(sums if CFG["t1"] == "sums" else rows_0))
    beside = [swap(t, "tensor", 1, inner) for t in terms_1]
    gates["beside"] = beside[:1]
    pieces_0 = spread(cross_0, "request", *gates[CFG["core0"]], own=rows_0 if CFG["own0"] else ())
    if CFG["hand"] == "t1":
        handed = place_blocks(after(ids, *terms_1), arrived)
    elif CFG["hand"] == "r1":
        handed = place_blocks(after(ids, *rows_1), arrived)
    terms_0 = terms_of(0, pieces_0, jnp.float32, split["t"], *([handed] if CFG["hand"] != "end" else []), *gates[CFG["t0"]], *terms_1)
    if CFG["hand"] == "end":
        handed = place_blocks(after(ids, *terms_0), arrived)
    across, beside = regroup(across, split["t"]), regroup(beside, split["t"])
    parts = len(split["t"])

    columns = {}
    earlier = []
    for part in CFG['tail'] if parts > 1 else [0]:
        summed = (after(terms_0[part], *(earlier if CFG['tie'] else [])) + beside[part] + across[part]).astype(sent)
        if inner > 1:
            summed = summed.reshape(rank_count, inner, share_rows, summed.shape[1]).swapaxes(0, 1)
            summed = lax.psum_scatter(
                summed, "tensor", scatter_dimension=0, axis_index_groups=groups, tiled=True
            )
        summed = summed.reshape(rank_count, share_rows, summed.shape[-1])
        earlier = [swap(summed[k], "request", k) for k in range(1, rank_count)]
        columns[part] = [summed[0]] + earlier
    ordered = [columns[part][k] for k in range(rank_count) for part in range(parts)]
    mixed = place_columns(ids, ordered, split['t'])[None]
    handed = handed.transpose(0, 2, 1)[None]
    return (mixed, handed)


def solution(mesh):
    placed = (
        P(("groups", "request"), "tensor"),
        P(("groups", "request"), "tensor"),
        P(("groups", "request"), "tensor", None),
        P("tensor", None, None),
        P("tensor", None, None),
        P("tensor", "request"),
        P(("groups", "request")),
        P(("groups", "request")),
        P(("groups", "request")),
        P(("groups", "request"), "tensor"),
    )
    return jax.shard_map(
        local,
        mesh=mesh,
        in_specs=placed,
        out_specs=(
            P(("groups", "request"), "tensor", None),
            P(("groups", "request"), None, "tensor", None),
        ),
        check_vma=False,
    )
```

```python
import functools
import math

import jax
import jax.numpy as jnp
from jax import lax
from jax.experimental import pallas as pl
from jax.experimental.pallas import tpu as pltpu
from jax.sharding import PartitionSpec as P

MIB = 1 << 20
LIGHT = pl.CostEstimate(flops=1, bytes_accessed=1, transcendentals=0)


def swap(value, axis, distance, inner=1):
    size = lax.axis_size(axis)
    pairs = [(i, ((i // inner) ^ distance) * inner + i % inner) for i in range(size)]
    return lax.ppermute(value, axis, pairs)


def after(value, *others):
    return lax.optimization_barrier((value, *others))[0]


def cross(values, axis):
    return [cross_one(value, axis) for value in values]


def spread(crossed, axis, *earlier, own=()):
    return [piece for pieces in crossed for piece in spread_one(pieces, axis, earlier, own)]


def cross_one(value, axis):
    pieces = {0: value}
    distance = lax.axis_size(axis) // 2
    while distance > 1:
        for k in list(pieces):
            pieces[k ^ distance] = swap(pieces[k], axis, distance)
        distance //= 2
    return pieces


def spread_one(pieces, axis, earlier, own):
    gates = {k: earlier if k else own for k in pieces}
    other = {k ^ 1: swap(after(v, *gates[k]), axis, 1) for k, v in pieces.items()}
    every = {**pieces, **other}
    return [every[k] for k in range(len(every))]


def part_of(size, wanted, unit=1):
    return max(d for d in range(unit, max(wanted, unit) + 1, unit) if size % d == 0)


def split_at(width, *places):
    edges = [0, *places, width]
    return [(a, b - a) for a, b in zip(edges, edges[1:]) if b > a]


def absorb_kernel(nope_ref, rope_ref, key_ref, out_ref):
    heads, latent, nope = key_ref.shape
    rotary = out_ref.shape[2] - latent
    for h in range(heads):
        out_ref[h, :, :latent] = lax.dot_general(
            nope_ref[:, h * nope : (h + 1) * nope],
            key_ref[h],
            (((1,), (1,)), ((), ())),
            preferred_element_type=jnp.float32,
        ).astype(out_ref.dtype)
        out_ref[h, :, latent:] = rope_ref[:, h * rotary : (h + 1) * rotary]


def absorb(q_nope, q_rope, w_key):
    rows = q_nope.shape[0]
    heads, latent, nope = w_key.shape
    rotary = q_rope.shape[1] // heads
    step = part_of(heads, 4, 2)
    return pl.pallas_call(
        absorb_kernel,
        grid=(heads // step,),
        in_specs=[
            pl.BlockSpec((rows, step * nope), lambda h: (0, h)),
            pl.BlockSpec((rows, step * rotary), lambda h: (0, h)),
            pl.BlockSpec((step, latent, nope), lambda h: (h, 0, 0)),
        ],
        out_specs=pl.BlockSpec((step, rows, latent + rotary), lambda h: (h, 0, 0)),
        out_shape=jax.ShapeDtypeStruct((heads, rows, latent + rotary), q_nope.dtype),
        compiler_params=pltpu.CompilerParams(vmem_limit_bytes=8 * MIB),
        cost_estimate=LIGHT,
        name="absorb",
    )(q_nope, q_rope, w_key)


def attend_kernel(
    distance, scale, ids_ref, prefix_ref, stretch_ref, query_ref, *refs
):
    block_refs, value_ref, out_refs, (keys, hidden) = refs[:4], refs[4], refs[5:-2], refs[-2:]
    heads, stretch, width = query_ref.shape
    each = pl.num_programs(0) // len(out_refs)
    latent, value_width = value_ref.shape[1:]
    part = block_refs[0].shape[2]
    span = 4 * part
    place = ids_ref[0]
    request = place ^ distance

    @pl.when(pl.program_id(0) == 0)
    def _():
        query_pos = prefix_ref[request] + lax.broadcasted_iota(jnp.int32, (stretch, part), 0)
        for k, ref in enumerate(block_refs):
            keys[:, k * part : (k + 1) * part] = ref[0]
            key_pos = (place ^ k) * part + lax.broadcasted_iota(jnp.int32, (stretch, part), 1)
            hidden[:, k * part : (k + 1) * part] = jnp.where(key_pos <= query_pos, 0.0, -1e30)

    query = query_ref[...].reshape(heads * stretch, width)
    scores = jnp.dot(query, keys[...], preferred_element_type=jnp.float32)
    scores = scores.reshape(heads, stretch, span) + hidden[...][None]
    top = jnp.max(scores, axis=2, keepdims=True)
    weights = jnp.exp2((scores - top) * (scale / math.log(2.0)))
    denom = jnp.sum(weights, axis=2, keepdims=True).reshape(heads * stretch, 1)
    latent_out = lax.dot_general(
        weights.astype(jnp.bfloat16).reshape(heads * stretch, span),
        keys[:latent],
        (((1,), (1,)), ((), ())),
        preferred_element_type=jnp.float32,
    )
    latent_out = (latent_out / denom).astype(jnp.bfloat16)
    live = lax.broadcasted_iota(jnp.int32, (stretch, value_width), 0) < stretch_ref[request]
    head_outs = []
    for h in range(heads):
        head_out = jnp.dot(
            latent_out[h * stretch : (h + 1) * stretch],
            value_ref[h],
            preferred_element_type=jnp.float32,
        )
        head_outs.append(jnp.where(live, head_out, 0.0).astype(out_refs[0].dtype))
    for part, out_ref in enumerate(out_refs):

        @pl.when(pl.program_id(0) // each == part)
        def _(out_ref=out_ref):
            for h in range(heads):
                out_ref[:, h * value_width : (h + 1) * value_width] = head_outs[h]


def attend(
    distance, ids, prefix_len, stretch_len, full_query, blocks, w_value, scale, halves
):
    heads, rows, width = full_query.shape
    latent, value_width = w_value.shape[1:]
    stretch = rows // prefix_len.shape[0]
    part = blocks[0].shape[2]
    step = part_of(heads // halves, 8)
    each = heads // halves // step
    span = 4 * part

    def half_of(half):
        return lambda h, *_: (0, jnp.clip(h - half * each, 0, each - 1))

    return pl.pallas_call(
        functools.partial(attend_kernel, distance, scale),
        grid_spec=pltpu.PrefetchScalarGridSpec(
            num_scalar_prefetch=3,
            grid=(heads // step,),
            in_specs=[
                pl.BlockSpec((step, stretch, width), lambda h, p, *_: (h, p[0] ^ distance, 0))
            ]
            + [pl.BlockSpec((1, width, part), lambda h, p, *_: ((p[0] ^ distance) % 2, 0, 0))] * 4
            + [pl.BlockSpec((step, latent, value_width), lambda h, *_: (h, 0, 0))],
            out_specs=[
                pl.BlockSpec((stretch, step * value_width), half_of(half)) for half in range(halves)
            ],
            scratch_shapes=[
                pltpu.VMEM((width, span), jnp.bfloat16),
                pltpu.VMEM((stretch, span), jnp.float32),
            ],
        ),
        out_shape=[jax.ShapeDtypeStruct((stretch, heads // halves * value_width), jnp.bfloat16)]
        * halves,
        compiler_params=pltpu.CompilerParams(vmem_limit_bytes=10 * MIB * max(span // 512, 1)),
        cost_estimate=LIGHT,
        name=f"attend_{distance}",
    )(ids, prefix_len, stretch_len, full_query, *blocks, w_value)


def project_kernel(stretch, splits, *refs):
    out_refs = refs[-1 - len(splits) : -1]
    weight_ref, rows = refs[-2 - len(splits)], refs[-1]
    row_refs = refs[: -2 - len(splits)]
    step = weight_ref.shape[1]
    n = pl.program_id(0)

    @pl.when(n == 0)
    def _():
        start = 0
        for ref in row_refs:
            line, column = start % rows.shape[0], start // rows.shape[0] * ref.shape[1]
            rows[line : line + stretch, column : column + ref.shape[1]] = ref[...]
            start += stretch

    total = jnp.dot(rows[...], weight_ref[...], preferred_element_type=jnp.float32)
    for (start, columns), out_ref in zip(splits, out_refs):

        @pl.when((n * step >= start) & (n * step < start + columns))
        def _(out_ref=out_ref):
            out_ref[...] = total.astype(out_ref.dtype)


def project(pieces, w_out, splits, dtype, name):
    stretch = pieces[0].shape[0]
    depth, width = w_out.shape
    rows = stretch * sum(piece.shape[1] for piece in pieces) // depth
    step = functools.reduce(math.gcd, [columns for _, columns in splits])
    step = part_of(step, 256, 128)

    def block_of(start, columns):
        last = columns // step - 1
        return lambda n: (0, jnp.clip(n - start // step, 0, last))

    return pl.pallas_call(
        functools.partial(project_kernel, stretch, splits),
        grid=(width // step,),
        in_specs=[pl.BlockSpec(piece.shape, lambda n: (0, 0)) for piece in pieces]
        + [pl.BlockSpec((depth, step), lambda n: (0, n))],
        out_specs=[pl.BlockSpec((rows, step), block_of(*split)) for split in splits],
        out_shape=[jax.ShapeDtypeStruct((rows, columns), dtype) for _, columns in splits],
        scratch_shapes=[pltpu.VMEM((rows, depth), jnp.bfloat16)],
        compiler_params=pltpu.CompilerParams(vmem_limit_bytes=14 * MIB),
        cost_estimate=LIGHT,
        name=name,
    )(*pieces, w_out)


SCALARS = pl.BlockSpec(memory_space=pltpu.SMEM)
WHOLE = pl.BlockSpec(memory_space=pltpu.VMEM)


def handoff_kernel(ids_ref, prefix_ref, stretch_ref, finished_ref, owner_ref, keys_ref, *outs):
    requests, width, block = keys_ref.shape
    pos = ids_ref[2] * block + lax.broadcasted_iota(jnp.int32, (width, block), 1)
    for k, out in enumerate(outs):
        chosen = jnp.zeros((width, block), jnp.float32)
        for q in range(requests):
            here = (finished_ref[q] > 0) & (owner_ref[q] == (ids_ref[1] ^ k))
            end = jnp.where(here, prefix_ref[q] + stretch_ref[q], 0)
            chosen = jnp.where(pos < end, keys_ref[q].astype(jnp.float32), chosen)
        out[...] = chosen.astype(out.dtype)


def handoff(ids, prefix_len, stretch_len, finished, owners, keys, rank_count):
    return pl.pallas_call(
        handoff_kernel,
        in_specs=[SCALARS] * 5 + [WHOLE],
        out_specs=[WHOLE] * rank_count,
        out_shape=[jax.ShapeDtypeStruct(keys.shape[1:], keys.dtype)] * rank_count,
        compiler_params=pltpu.CompilerParams(vmem_limit_bytes=8 * MIB),
        name="handoff",
    )(ids, prefix_len, stretch_len, finished, owners, keys)


def place_blocks_kernel(ids_ref, *refs):
    out = refs[-1]
    for k, ref in enumerate(refs[:-1]):
        out[ids_ref[1] ^ k] = ref[...]


def place_blocks(ids, pieces):
    return pl.pallas_call(
        place_blocks_kernel,
        in_specs=[SCALARS] + [WHOLE] * len(pieces),
        out_specs=WHOLE,
        out_shape=jax.ShapeDtypeStruct((len(pieces), *pieces[0].shape), pieces[0].dtype),
        compiler_params=pltpu.CompilerParams(vmem_limit_bytes=8 * MIB),
        name="place_blocks",
    )(ids, *pieces)


def place_columns_kernel(splits, ids_ref, *refs):
    out = refs[-1]
    width = sum(columns for _, columns in splits)
    for n, ref in enumerate(refs[:-1]):
        k, part = divmod(n, len(splits))
        start, columns = splits[part]
        start = pl.multiple_of((ids_ref[1] ^ k) * width + start, 128)
        out[:, pl.ds(start, columns)] = ref[...]


def place_columns(ids, pieces, splits):
    rows = pieces[0].shape[0]
    width = sum(piece.shape[1] for piece in pieces)
    return pl.pallas_call(
        functools.partial(place_columns_kernel, splits),
        in_specs=[SCALARS] + [WHOLE] * len(pieces),
        out_specs=WHOLE,
        out_shape=jax.ShapeDtypeStruct((rows, width), pieces[0].dtype),
        compiler_params=pltpu.CompilerParams(vmem_limit_bytes=8 * MIB),
        name="place_columns",
    )(ids, *pieces)


def local(
    q_nope, q_rope, latent_keys, w_key, w_value, w_out, prefix_len, stretch_len, finished, owners
):
    request_count = prefix_len.shape[0]
    row_count = q_nope.shape[0]
    head_count, latent_width, nope_width = w_key.shape
    rotary_width = q_rope.shape[1] // head_count
    score_scale = (nope_width + rotary_width) ** (-0.5)
    rank_count = lax.axis_size("request")
    tensor_count = lax.axis_size("tensor")
    inner = tensor_count // request_count
    share_rows = row_count // tensor_count
    rank = lax.axis_index("request")
    place = lax.axis_index("tensor")
    outer_place = place // inner
    ids = jnp.stack([outer_place, rank, place]).astype(jnp.int32)

    block_keys = latent_keys.transpose(0, 2, 1)
    if inner > 1:
        groups = [[o * inner + i for i in range(inner)] for o in range(request_count)]
        own_keys = lax.all_gather(
            block_keys, "tensor", axis=2, tiled=True, axis_index_groups=groups
        )
    else:
        own_keys = block_keys
    near = (outer_place // 2) * 2
    near_keys = lax.dynamic_slice_in_dim(own_keys, near, 2, 0)
    far_keys = lax.dynamic_slice_in_dim(own_keys, near ^ 2, 2, 0)
    far_two = swap(near_keys, "tensor", 2, inner)
    far_one = swap(far_keys, "tensor", 1, inner)

    outgoing = handoff(
        after(ids, far_keys, near_keys),
        prefix_len,
        stretch_len,
        finished,
        owners.reshape(request_count),
        block_keys,
        rank_count,
    )
    full_query = absorb(after(q_nope, *outgoing), q_rope, w_key)
    arrived = [outgoing[0]] + [
        swap(after(outgoing[k], full_query), "request", k) for k in range(1, rank_count)
    ]
    far_three = swap(after(far_two, far_one, full_query), "tensor", 1, inner)
    near_two = swap(after(far_keys, far_three), "tensor", 2, inner)
    near_one = swap(after(near_keys, far_three), "tensor", 1, inner)
    far_blocks = [far_keys, far_one, far_two, far_three]
    near_blocks = [near_keys, near_one, near_two]

    halves = 2 if head_count % 2 == 0 else 1

    def rows_of(distance, blocks, *earlier):
        return attend(
            distance,
            after(ids, *earlier),
            prefix_len,
            stretch_len,
            full_query,
            blocks,
            w_value,
            score_scale,
            halves,
        )

    width = w_out.shape[1]
    splits = split_at(width, -(-width // 512) * 256) if width % 256 == 0 else split_at(width)
    sent = jnp.bfloat16

    def terms_of(distance, pieces, dtype, *earlier):
        pieces = [after(pieces[0], *earlier)] + pieces[1:]
        return project(pieces, w_out, splits, dtype, f"project_{distance}")

    rows_3 = rows_of(3, far_blocks, *arrived)
    cross_3 = cross(rows_3, "request")
    rows_2 = rows_of(2, far_blocks, *rows_3)
    cross_2 = cross(rows_2, "request")
    pieces_3 = spread(cross_3, "request", *rows_2, near_one, near_two, own=rows_2)
    terms_3 = terms_of(3, pieces_3, sent, *rows_2)
    near_blocks.append(swap(near_two, "tensor", 1, inner))
    opposite = [swap(after(t, near_blocks[3]), "tensor", 1, inner) for t in terms_3]
    rows_1 = rows_of(1, near_blocks, *terms_3)
    cross_1 = cross(rows_1, "request")
    pieces_2 = spread(cross_2[:1], "request")
    pieces_2 += spread(cross_2[1:], "request", *rows_1)
    terms_2 = terms_of(2, pieces_2, jnp.float32, *rows_1)
    sums = [(t + o).astype(sent) for t, o in zip(terms_2, opposite)]
    across = [swap(t, "tensor", 2, inner) for t in sums]
    rows_0 = rows_of(0, near_blocks, *sums)
    cross_0 = cross(rows_0, "request")
    pieces_1 = spread(cross_1, "request", *sums)
    terms_1 = terms_of(1, pieces_1, sent, *sums)
    beside = [swap(t, "tensor", 1, inner) for t in terms_1]
    pieces_0 = spread(cross_0, "request", across[0], own=rows_0)
    terms_0 = terms_of(0, pieces_0, jnp.float32, *terms_1)
    handed = place_blocks(after(ids, *terms_0), arrived)

    columns = []
    earlier = []
    for kept_terms, near_terms, far_terms in zip(terms_0, beside, across):
        summed = (after(kept_terms, *earlier) + near_terms + far_terms).astype(sent)
        if inner > 1:
            summed = summed.reshape(rank_count, inner, share_rows, summed.shape[1]).swapaxes(0, 1)
            summed = lax.psum_scatter(
                summed, "tensor", scatter_dimension=0, axis_index_groups=groups, tiled=True
            )
        summed = summed.reshape(rank_count, share_rows, summed.shape[-1])
        earlier = [swap(summed[k], "request", k) for k in range(1, rank_count)]
        columns.append([summed[0]] + earlier)
    ordered = [part[k] for k in range(rank_count) for part in columns]
    mixed = place_columns(ids, ordered, splits)[None]
    handed = handed.transpose(0, 2, 1)[None]
    return (mixed, handed)


def solution(mesh):
    placed = (
        P(("groups", "request"), "tensor"),
        P(("groups", "request"), "tensor"),
        P(("groups", "request"), "tensor", None),
        P("tensor", None, None),
        P("tensor", None, None),
        P("tensor", "request"),
        P(("groups", "request")),
        P(("groups", "request")),
        P(("groups", "request")),
        P(("groups", "request"), "tensor"),
    )
    return jax.shard_map(
        local,
        mesh=mesh,
        in_specs=placed,
        out_specs=(
            P(("groups", "request"), "tensor", None),
            P(("groups", "request"), None, "tensor", None),
        ),
        check_vma=False,
    )
```

```python
import functools
import math

import jax
import jax.numpy as jnp
from jax import lax
from jax.experimental import pallas as pl
from jax.experimental.pallas import tpu as pltpu
from jax.sharding import PartitionSpec as P

MIB = 1 << 20
LIGHT = pl.CostEstimate(flops=1, bytes_accessed=1, transcendentals=0)


def swap(value, axis, distance, inner=1):
    size = lax.axis_size(axis)
    pairs = [(i, ((i // inner) ^ distance) * inner + i % inner) for i in range(size)]
    return lax.ppermute(value, axis, pairs)


def after(value, *others):
    return lax.optimization_barrier((value, *others))[0]


def cross(values, axis):
    return [cross_one(value, axis) for value in values]


def spread(crossed, axis, *earlier, own=()):
    return [piece for pieces in crossed for piece in spread_one(pieces, axis, earlier, own)]


def cross_one(value, axis):
    pieces = {0: value}
    distance = lax.axis_size(axis) // 2
    while distance > 1:
        for k in list(pieces):
            pieces[k ^ distance] = swap(pieces[k], axis, distance)
        distance //= 2
    return pieces


def spread_one(pieces, axis, earlier, own):
    gates = {k: earlier if k else own for k in pieces}
    other = {k ^ 1: swap(after(v, *gates[k]), axis, 1) for k, v in pieces.items()}
    every = {**pieces, **other}
    return [every[k] for k in range(len(every))]


def part_of(size, wanted, unit=1):
    return max(d for d in range(unit, max(wanted, unit) + 1, unit) if size % d == 0)


def split_at(width, *places):
    edges = [0, *places, width]
    return [(a, b - a) for a, b in zip(edges, edges[1:]) if b > a]


def absorb_kernel(nope_ref, rope_ref, key_ref, out_ref):
    heads, latent, nope = key_ref.shape
    rotary = out_ref.shape[2] - latent
    for h in range(heads):
        out_ref[h, :, :latent] = lax.dot_general(
            nope_ref[:, h * nope : (h + 1) * nope],
            key_ref[h],
            (((1,), (1,)), ((), ())),
            preferred_element_type=jnp.float32,
        ).astype(out_ref.dtype)
        out_ref[h, :, latent:] = rope_ref[:, h * rotary : (h + 1) * rotary]


def absorb(q_nope, q_rope, w_key):
    rows = q_nope.shape[0]
    heads, latent, nope = w_key.shape
    rotary = q_rope.shape[1] // heads
    step = part_of(heads, 4, 2)
    return pl.pallas_call(
        absorb_kernel,
        grid=(heads // step,),
        in_specs=[
            pl.BlockSpec((rows, step * nope), lambda h: (0, h)),
            pl.BlockSpec((rows, step * rotary), lambda h: (0, h)),
            pl.BlockSpec((step, latent, nope), lambda h: (h, 0, 0)),
        ],
        out_specs=pl.BlockSpec((step, rows, latent + rotary), lambda h: (h, 0, 0)),
        out_shape=jax.ShapeDtypeStruct((heads, rows, latent + rotary), q_nope.dtype),
        compiler_params=pltpu.CompilerParams(vmem_limit_bytes=8 * MIB),
        cost_estimate=LIGHT,
        name="absorb",
    )(q_nope, q_rope, w_key)


def attend_kernel(
    distance, scale, ids_ref, prefix_ref, stretch_ref, query_ref, *refs
):
    block_refs, value_ref, out_refs, (keys, hidden) = refs[:4], refs[4], refs[5:-2], refs[-2:]
    heads, stretch, width = query_ref.shape
    each = pl.num_programs(0) // len(out_refs)
    latent, value_width = value_ref.shape[1:]
    part = block_refs[0].shape[2]
    span = 4 * part
    place = ids_ref[0]
    request = place ^ distance

    @pl.when(pl.program_id(0) == 0)
    def _():
        query_pos = prefix_ref[request] + lax.broadcasted_iota(jnp.int32, (stretch, part), 0)
        for k, ref in enumerate(block_refs):
            keys[:, k * part : (k + 1) * part] = ref[0]
            key_pos = (place ^ k) * part + lax.broadcasted_iota(jnp.int32, (stretch, part), 1)
            hidden[:, k * part : (k + 1) * part] = jnp.where(key_pos <= query_pos, 0.0, -1e30)

    query = query_ref[...].reshape(heads * stretch, width)
    scores = jnp.dot(query, keys[...], preferred_element_type=jnp.float32)
    scores = scores.reshape(heads, stretch, span) + hidden[...][None]
    top = jnp.max(scores, axis=2, keepdims=True)
    weights = jnp.exp2((scores - top) * (scale / math.log(2.0)))
    denom = jnp.sum(weights, axis=2, keepdims=True).reshape(heads * stretch, 1)
    latent_out = lax.dot_general(
        weights.astype(jnp.bfloat16).reshape(heads * stretch, span),
        keys[:latent],
        (((1,), (1,)), ((), ())),
        preferred_element_type=jnp.float32,
    )
    latent_out = (latent_out / denom).astype(jnp.bfloat16)
    live = lax.broadcasted_iota(jnp.int32, (stretch, value_width), 0) < stretch_ref[request]
    head_outs = []
    for h in range(heads):
        head_out = jnp.dot(
            latent_out[h * stretch : (h + 1) * stretch],
            value_ref[h],
            preferred_element_type=jnp.float32,
        )
        head_outs.append(jnp.where(live, head_out, 0.0).astype(out_refs[0].dtype))
    for part, out_ref in enumerate(out_refs):

        @pl.when(pl.program_id(0) // each == part)
        def _(out_ref=out_ref):
            for h in range(heads):
                out_ref[:, h * value_width : (h + 1) * value_width] = head_outs[h]


def attend(
    distance, ids, prefix_len, stretch_len, full_query, blocks, w_value, scale, halves
):
    heads, rows, width = full_query.shape
    latent, value_width = w_value.shape[1:]
    stretch = rows // prefix_len.shape[0]
    part = blocks[0].shape[2]
    step = part_of(heads // halves, 8)
    each = heads // halves // step
    span = 4 * part

    def half_of(half):
        return lambda h, *_: (0, jnp.clip(h - half * each, 0, each - 1))

    return pl.pallas_call(
        functools.partial(attend_kernel, distance, scale),
        grid_spec=pltpu.PrefetchScalarGridSpec(
            num_scalar_prefetch=3,
            grid=(heads // step,),
            in_specs=[
                pl.BlockSpec((step, stretch, width), lambda h, p, *_: (h, p[0] ^ distance, 0))
            ]
            + [pl.BlockSpec((1, width, part), lambda h, p, *_: ((p[0] ^ distance) % 2, 0, 0))] * 4
            + [pl.BlockSpec((step, latent, value_width), lambda h, *_: (h, 0, 0))],
            out_specs=[
                pl.BlockSpec((stretch, step * value_width), half_of(half)) for half in range(halves)
            ],
            scratch_shapes=[
                pltpu.VMEM((width, span), jnp.bfloat16),
                pltpu.VMEM((stretch, span), jnp.float32),
            ],
        ),
        out_shape=[jax.ShapeDtypeStruct((stretch, heads // halves * value_width), jnp.bfloat16)]
        * halves,
        compiler_params=pltpu.CompilerParams(vmem_limit_bytes=10 * MIB * max(span // 512, 1)),
        cost_estimate=LIGHT,
        name=f"attend_{distance}",
    )(ids, prefix_len, stretch_len, full_query, *blocks, w_value)


def project_kernel(stretch, splits, *refs):
    out_refs = refs[-1 - len(splits) : -1]
    weight_ref, rows = refs[-2 - len(splits)], refs[-1]
    row_refs = refs[: -2 - len(splits)]
    step = weight_ref.shape[1]
    n = pl.program_id(0)

    @pl.when(n == 0)
    def _():
        start = 0
        for ref in row_refs:
            line, column = start % rows.shape[0], start // rows.shape[0] * ref.shape[1]
            rows[line : line + stretch, column : column + ref.shape[1]] = ref[...]
            start += stretch

    total = jnp.dot(rows[...], weight_ref[...], preferred_element_type=jnp.float32)
    for (start, columns), out_ref in zip(splits, out_refs):

        @pl.when((n * step >= start) & (n * step < start + columns))
        def _(out_ref=out_ref):
            out_ref[...] = total.astype(out_ref.dtype)


def project(pieces, w_out, splits, dtype, name):
    stretch = pieces[0].shape[0]
    depth, width = w_out.shape
    rows = stretch * sum(piece.shape[1] for piece in pieces) // depth
    step = functools.reduce(math.gcd, [columns for _, columns in splits])
    step = part_of(step, 256, 128)

    def block_of(start, columns):
        last = columns // step - 1
        return lambda n: (0, jnp.clip(n - start // step, 0, last))

    return pl.pallas_call(
        functools.partial(project_kernel, stretch, splits),
        grid=(width // step,),
        in_specs=[pl.BlockSpec(piece.shape, lambda n: (0, 0)) for piece in pieces]
        + [pl.BlockSpec((depth, step), lambda n: (0, n))],
        out_specs=[pl.BlockSpec((rows, step), block_of(*split)) for split in splits],
        out_shape=[jax.ShapeDtypeStruct((rows, columns), dtype) for _, columns in splits],
        scratch_shapes=[pltpu.VMEM((rows, depth), jnp.bfloat16)],
        compiler_params=pltpu.CompilerParams(vmem_limit_bytes=14 * MIB),
        cost_estimate=LIGHT,
        name=name,
    )(*pieces, w_out)


SCALARS = pl.BlockSpec(memory_space=pltpu.SMEM)
WHOLE = pl.BlockSpec(memory_space=pltpu.VMEM)


def handoff_kernel(ids_ref, prefix_ref, stretch_ref, finished_ref, owner_ref, keys_ref, *outs):
    requests, width, block = keys_ref.shape
    pos = ids_ref[2] * block + lax.broadcasted_iota(jnp.int32, (width, block), 1)
    for k, out in enumerate(outs):
        chosen = jnp.zeros((width, block), jnp.float32)
        for q in range(requests):
            here = (finished_ref[q] > 0) & (owner_ref[q] == (ids_ref[1] ^ k))
            end = jnp.where(here, prefix_ref[q] + stretch_ref[q], 0)
            chosen = jnp.where(pos < end, keys_ref[q].astype(jnp.float32), chosen)
        out[...] = chosen.astype(out.dtype)


def handoff(ids, prefix_len, stretch_len, finished, owners, keys, rank_count):
    return pl.pallas_call(
        handoff_kernel,
        in_specs=[SCALARS] * 5 + [WHOLE],
        out_specs=[WHOLE] * rank_count,
        out_shape=[jax.ShapeDtypeStruct(keys.shape[1:], keys.dtype)] * rank_count,
        compiler_params=pltpu.CompilerParams(vmem_limit_bytes=8 * MIB),
        name="handoff",
    )(ids, prefix_len, stretch_len, finished, owners, keys)


def place_blocks_kernel(ids_ref, *refs):
    out = refs[-1]
    for k, ref in enumerate(refs[:-1]):
        out[ids_ref[1] ^ k] = ref[...]


def place_blocks(ids, pieces):
    return pl.pallas_call(
        place_blocks_kernel,
        in_specs=[SCALARS] + [WHOLE] * len(pieces),
        out_specs=WHOLE,
        out_shape=jax.ShapeDtypeStruct((len(pieces), *pieces[0].shape), pieces[0].dtype),
        compiler_params=pltpu.CompilerParams(vmem_limit_bytes=8 * MIB),
        name="place_blocks",
    )(ids, *pieces)


def place_columns_kernel(splits, ids_ref, *refs):
    out = refs[-1]
    width = sum(columns for _, columns in splits)
    for n, ref in enumerate(refs[:-1]):
        k, part = divmod(n, len(splits))
        start, columns = splits[part]
        start = pl.multiple_of((ids_ref[1] ^ k) * width + start, 128)
        out[:, pl.ds(start, columns)] = ref[...]


def place_columns(ids, pieces, splits):
    rows = pieces[0].shape[0]
    width = sum(piece.shape[1] for piece in pieces)
    return pl.pallas_call(
        functools.partial(place_columns_kernel, splits),
        in_specs=[SCALARS] + [WHOLE] * len(pieces),
        out_specs=WHOLE,
        out_shape=jax.ShapeDtypeStruct((rows, width), pieces[0].dtype),
        compiler_params=pltpu.CompilerParams(vmem_limit_bytes=8 * MIB),
        name="place_columns",
    )(ids, *pieces)


def local(
    q_nope, q_rope, latent_keys, w_key, w_value, w_out, prefix_len, stretch_len, finished, owners
):
    request_count = prefix_len.shape[0]
    row_count = q_nope.shape[0]
    head_count, latent_width, nope_width = w_key.shape
    rotary_width = q_rope.shape[1] // head_count
    score_scale = (nope_width + rotary_width) ** (-0.5)
    rank_count = lax.axis_size("request")
    tensor_count = lax.axis_size("tensor")
    inner = tensor_count // request_count
    share_rows = row_count // tensor_count
    rank = lax.axis_index("request")
    place = lax.axis_index("tensor")
    outer_place = place // inner
    ids = jnp.stack([outer_place, rank, place]).astype(jnp.int32)

    block_keys = latent_keys.transpose(0, 2, 1)
    if inner > 1:
        groups = [[o * inner + i for i in range(inner)] for o in range(request_count)]
        own_keys = lax.all_gather(
            block_keys, "tensor", axis=2, tiled=True, axis_index_groups=groups
        )
    else:
        own_keys = block_keys
    near = (outer_place // 2) * 2
    near_keys = lax.dynamic_slice_in_dim(own_keys, near, 2, 0)
    far_keys = lax.dynamic_slice_in_dim(own_keys, near ^ 2, 2, 0)
    far_two = swap(near_keys, "tensor", 2, inner)
    far_one = swap(far_keys, "tensor", 1, inner)

    outgoing = handoff(
        after(ids, far_keys, near_keys),
        prefix_len,
        stretch_len,
        finished,
        owners.reshape(request_count),
        block_keys,
        rank_count,
    )
    full_query = absorb(after(q_nope, *outgoing), q_rope, w_key)
    arrived = [outgoing[0]] + [
        swap(after(outgoing[k], full_query), "request", k) for k in range(1, rank_count)
    ]
    far_three = swap(after(far_two, far_one, full_query), "tensor", 1, inner)
    near_two = swap(after(far_keys, far_three), "tensor", 2, inner)
    near_one = swap(after(near_keys, far_three), "tensor", 1, inner)
    far_blocks = [far_keys, far_one, far_two, far_three]
    near_blocks = [near_keys, near_one, near_two]

    halves = 2 if head_count % 2 == 0 else 1

    def rows_of(distance, blocks, *earlier):
        return attend(
            distance,
            after(ids, *earlier),
            prefix_len,
            stretch_len,
            full_query,
            blocks,
            w_value,
            score_scale,
            halves,
        )

    width = w_out.shape[1]
    splits = split_at(width, -(-width // 512) * 256) if width % 256 == 0 else split_at(width)
    sent = jnp.bfloat16

    def terms_of(distance, pieces, dtype, *earlier):
        pieces = [after(pieces[0], *earlier)] + pieces[1:]
        return project(pieces, w_out, splits, dtype, f"project_{distance}")

    rows_3 = rows_of(3, far_blocks, *arrived)
    cross_3 = cross(rows_3, "request")
    rows_2 = rows_of(2, far_blocks, *rows_3)
    cross_2 = cross(rows_2, "request")
    pieces_3 = spread(cross_3, "request", *rows_2, near_one, near_two, own=rows_2)
    terms_3 = terms_of(3, pieces_3, sent, *rows_2)
    near_blocks.append(swap(near_two, "tensor", 1, inner))
    opposite = [swap(after(t, near_blocks[3]), "tensor", 1, inner) for t in terms_3]
    rows_1 = rows_of(1, near_blocks, *terms_3, *cross_2[0].values())
    cross_1 = cross(rows_1, "request")
    pieces_2 = spread(cross_2[:1], "request")
    pieces_2 += spread(cross_2[1:], "request", *rows_1)
    terms_2 = terms_of(2, pieces_2, jnp.float32, *rows_1)
    sums = [(t + o).astype(sent) for t, o in zip(terms_2, opposite)]
    across = [swap(t, "tensor", 2, inner) for t in sums]
    rows_0 = rows_of(0, near_blocks, *sums)
    cross_0 = cross(rows_0, "request")
    pieces_1 = spread(cross_1, "request", *sums)
    terms_1 = terms_of(1, pieces_1, sent, *sums)
    beside = [swap(t, "tensor", 1, inner) for t in terms_1]
    pieces_0 = spread(cross_0, "request", across[0], own=rows_0)
    terms_0 = terms_of(0, pieces_0, jnp.float32)
    handed = place_blocks(after(ids, *terms_0), arrived)

    columns = []
    earlier = []
    for kept_terms, near_terms, far_terms in zip(terms_0, beside, across):
        summed = (after(kept_terms, *earlier) + near_terms + far_terms).astype(sent)
        if inner > 1:
            summed = summed.reshape(rank_count, inner, share_rows, summed.shape[1]).swapaxes(0, 1)
            summed = lax.psum_scatter(
                summed, "tensor", scatter_dimension=0, axis_index_groups=groups, tiled=True
            )
        summed = summed.reshape(rank_count, share_rows, summed.shape[-1])
        earlier = [swap(summed[k], "request", k) for k in range(1, rank_count)]
        columns.append([summed[0]] + earlier)
    ordered = [part[k] for k in range(rank_count) for part in columns]
    mixed = place_columns(ids, ordered, splits)[None]
    handed = handed.transpose(0, 2, 1)[None]
    return (mixed, handed)


def solution(mesh):
    placed = (
        P(("groups", "request"), "tensor"),
        P(("groups", "request"), "tensor"),
        P(("groups", "request"), "tensor", None),
        P("tensor", None, None),
        P("tensor", None, None),
        P("tensor", "request"),
        P(("groups", "request")),
        P(("groups", "request")),
        P(("groups", "request")),
        P(("groups", "request"), "tensor"),
    )
    return jax.shard_map(
        local,
        mesh=mesh,
        in_specs=placed,
        out_specs=(
            P(("groups", "request"), "tensor", None),
            P(("groups", "request"), None, "tensor", None),
        ),
        check_vma=False,
    )
```
